256 devices in a mesh: row: 32 (over y, z), col: 8 (over x, core).
Axes of the slice: x: 4, y: 4, z: 8, core: 2. Of those that a mesh axis runs over, the one named last changes fastest.
Arguments:
- iterate: float32 [2048, 7168], P('row', 'col'), may hold values from -1 to 1
Outputs:
- update: float32 [2048, 7168], P('row', 'col')
The draws below stay inside these ranges and needn't reach their ends.
All inputs are finite; a program needn't handle non-finite values.
Results may differ from the reference program's by a relative error of at most 0.00005.
Values sent between devices are 32-bit elements; how exact they have to be, the bound alone decides.
A program may use at most 64 MiB of HBM per device.

```python
import math
import jax
import jax.numpy as jnp
from jax import lax

M = 2048
N = 7168


def draw_iterate(key, part):
    key = jax.random.fold_in(key, 11)
    entry_key, row_key, column_key = jax.random.split(key, 3)
    positions = jnp.arange(M, dtype=jnp.float32) / M
    entries = jax.random.truncated_normal(entry_key, -6.0, 6.0, (M, N), jnp.float32)
    ramp_scale = 3.0 ** (positions - 1.0)
    overall = 1.6
    row_scale = jnp.exp(jax.random.uniform(row_key, (M, 1), jnp.float32, -2.3025851, 0.0))
    column_scale = jnp.exp(jax.random.uniform(column_key, (1, N), jnp.float32, -2.3025851, 0.0))
    return overall * ramp_scale[:, None] * row_scale * column_scale * entries / math.sqrt(N)


def setup_inputs(seed: int = 0) -> dict:
    splits = jax.random.split(jax.random.key(seed), 2)
    return {
        "iterate": draw_iterate(jax.random.fold_in(splits[1], 71), 0),
    }


LINEAR_TERM = 3.4445
CUBIC_TERM = -4.775
QUINTIC_TERM = 2.0315
TARGET_SCALE = 0.2
EPSILON = 1e-07
PRECISE = lax.Precision.HIGHEST

def product(left, right):
    return jnp.dot(left, right, precision=PRECISE, preferred_element_type=jnp.float32)

def reference(iterate):
    gram_matrix = product(iterate, iterate.T)
    polynomial_rows = CUBIC_TERM * gram_matrix + QUINTIC_TERM * product(gram_matrix, gram_matrix)
    polar_rows = LINEAR_TERM * iterate + product(polynomial_rows, iterate)
    squares = jnp.sum(polar_rows * polar_rows)
    return TARGET_SCALE * polar_rows / jnp.sqrt(squares / (M * N) + EPSILON)
```

```python
import functools
import jax
import jax.numpy as jnp
from jax import lax
from jax.experimental import pallas as pl
from jax.experimental.pallas import tpu as pltpu
from jax.sharding import PartitionSpec as P

M = 2048
N = 7168
NY = 4
NZ = 8
X_PARTS = 4

LINEAR_TERM = 3.4445
CUBIC_TERM = -4.775
QUINTIC_TERM = 2.0315
TARGET_SCALE = 0.2
EPSILON = 1e-07
MESH = pl.DeviceIdType.MESH
F32 = jnp.float32
BF16 = jnp.bfloat16


def split(value):
    high = value.astype(BF16)
    return high, (value - high.astype(F32)).astype(BF16)


def dot3(left, right, left_dim, right_dim):
    return lax.dot_general(
        jnp.concatenate([left[0], left[0], left[1]], axis=left_dim),
        jnp.concatenate([right[0], right[1], right[0]], axis=right_dim),
        (((left_dim,), (right_dim,)), ((), ())),
        preferred_element_type=F32,
    )


class Ring:
    def __init__(self, n, parts, device, src, land, two, every, send_sem, recv_sem):
        self.parts, self.device, self.src, self.land = parts, device, src, land
        self.two, self.every, self.send_sem, self.recv_sem = two, every, send_sem, recv_sem
        self.items = ring_items(n, parts)

    def copy(self, src, dst, t, way):
        return pltpu.make_async_remote_copy(
            src_ref=src,
            dst_ref=dst,
            send_sem=self.send_sem,
            recv_sem=self.recv_sem.at[t],
            device_id=self.device(way),
            device_id_type=MESH,
        )

    def send(self, t):
        for way in (1, -1):
            d, h = t // self.parts, t % self.parts
            h = h if way > 0 else self.parts - 1 - h
            self.copy(self.src(way, d, h), self.land(way, d, h), t, way).start()

    def open(self):
        for t in range(min(self.parts, self.items)):
            self.send(t)

    def take(self, t):
        self.copy(self.two, self.two, t, 1).wait_recv()
        if t + self.parts < self.items:
            self.send(t + self.parts)

    def close(self):
        self.copy(self.every, self.every, 0, 1).wait_send()


def ring_items(n, parts):
    return parts * (n - 1) // 2


def slot_order(n):
    out = [0]
    for s in range(1, n // 2):
        out += [s, n - s]
    return out + [n // 2]


def kernel(
    nc, x_hbm, out_ref,
    xv, xz, xy, xhi, xlo, jhi, jlo, gp, gr, gs, gy, gj, tt, tz, thi, tlo, cp, cr, pp, qy, qk, pthi, ptlo, op, ry,
    sq, sqx, sqz, sqy,
    x_s, xz_s, xz_r, xy_s, xy_r, g_s, g_r, gy_s, gy_r, tz_s, tz_r, c_s, c_r, u_s, u_r, v_s, v_r, p_s, p_r, qk_s, qk_r, ry_s, ry_r,
    qx_s, qx_r, qz_s, qz_r, qy_s, qy_r,
):
    rows, width = xv.shape
    half = rows // 2
    sub = rows // nc
    owned = NZ * sub
    wide = NY * rows
    row, col = lax.axis_index("row"), lax.axis_index("col")
    y, z = lax.div(row, NZ), lax.rem(row, NZ)

    def at_y(step):
        return (lax.rem(y + step + NY, NY) * NZ + z, col)

    def at_z(step):
        return (y * NZ + lax.rem(z + step + NZ, NZ), col)

    nx = nc // 2
    x, core = lax.div(col, 2), lax.rem(col, 2)
    twin = (row, col + 1 - 2 * core)

    def at_x(step):
        return (row, lax.rem(x + step + nx, nx) * 2 + core)

    def at_col(step):
        return (row, lax.rem(col + step, nc))

    def copy(src, dst, send_sem, recv_sem, device):
        return pltpu.make_async_remote_copy(
            src_ref=src, dst_ref=dst, send_sem=send_sem, recv_sem=recv_sem, device_id=device, device_id_type=MESH
        )

    fetch = pltpu.make_async_copy(x_hbm, xv, x_s)
    fetch.start()
    barrier = pltpu.get_barrier_semaphore()
    friends = [at_z(1), at_z(-1), at_y(1), at_y(-1), at_y(2)]
    friends += [at_z(s) for s in range(2, NZ - 1)] + [at_col(s) for s in range(1, nc)]
    for friend in friends:
        pl.semaphore_signal(barrier, inc=1, device_id=friend, device_id_type=MESH)
    pl.semaphore_wait(barrier, len(friends))

    def halves(h):
        return pl.ds(h * half, half)

    def block_ring(n, parts, device, own, buf, send_sem, recv_sem):
        def src(way, d, h):
            return own(h) if d == 0 else buf.at[way * d % n, pl.ds(h * (rows // parts), rows // parts)]

        def land(way, d, h):
            return buf.at[way * (d + 1) % n, pl.ds(h * (rows // parts), rows // parts)]

        two = buf.at[0, pl.ds(0, 2 * (rows // parts))]
        return Ring(n, parts, device, src, land, two, buf.at[pl.ds(0, n - 1)], send_sem, recv_sem)

    def own_x(h):
        return x_hbm.at[pl.ds(h * (rows // X_PARTS), rows // X_PARTS)]

    z_ring = block_ring(NZ, X_PARTS, at_z, own_x, xz, xz_s, xz_r)
    y_ring = block_ring(NY, X_PARTS, at_y, own_x, xy, xy_s, xy_r)
    z_ring.open()
    y_ring.open()
    fetch.wait()
    order = slot_order(NZ)
    closing = []

    def span(first, last):
        return pl.ds(first * rows, (last - first) * rows)

    def keep_j(slot, value):
        where = pl.ds(pl.multiple_of(lax.rem(y - slot + NY, NY) * rows, rows), rows)
        hi, lo = split(value)
        jhi[where, :] = hi
        jlo[where, :] = lo

    def keep_i(pos, value):
        hi, lo = split(value)
        xhi[span(pos, pos + 1), :] = hi
        xlo[span(pos, pos + 1), :] = lo

    def each(n, act):
        for j in sorted(range(1, n), key=lambda j: -min(j, n - j)):
            act(j)

    def fan(n, whole, send_sem, recv_sem, make):
        every = copy(whole, whole, send_sem, recv_sem, twin)
        each(n, lambda j: copy(*make(j)[:2], send_sem, recv_sem, make(j)[2]).start())
        closing.append(every.wait_send)
        return every.wait_recv

    def scatter(part, buf, b, first, last, send_sem, recv_sem):
        def make(j):
            to = at_col(j)
            mine_there = pl.ds(pl.multiple_of(to[1] * sub, sub), sub)
            return part.at[pl.ds(first, last - first), mine_there], buf.at[j - 1, pl.ds(first, last - first)], to

        return fan(nc, buf.at[:, pl.ds(first, last - first)], send_sem.at[b], recv_sem.at[b], make)

    def gathered(part, buf, pos):
        total = part[pos, pl.ds(pl.multiple_of(col * sub, sub), sub), :]
        for j in range(1, nc):
            total = total + buf[j - 1, pos]
        return total

    def spread_y(src, buf, b, first, last, send_sem, recv_sem):
        where = pl.ds(first, last - first)
        return fan(
            NY, buf.at[:, where], send_sem.at[b], recv_sem.at[b], lambda s: (src, buf.at[s - 1, where], at_y(s))
        )

    keep_i(0, xv[...])
    keep_j(0, xv[...])
    y_waits, arrivals = [], []
    spans = ((0, 5), (5, NZ))

    def gram(first, last):
        for pos in range(first, last):
            if pos:
                keep_i(pos, xz[order[pos]])
        where = span(first, last)
        block = dot3((xhi[where, :], xlo[where, :]), (jhi[...], jlo[...]), 1, 1)
        gp[first:last] = block.reshape(last - first, rows, wide)

    y_spans = ((0, 4), (4, 7), (7, NZ))

    def drain_g(b, which):
        first, last = y_spans[b]
        for one in which:
            arrivals[one]()
        for pos in range(first, last):
            gs[pos] = gathered(gp, gr, pos)
        y_waits.append(spread_y(gs.at[pl.ds(first, last - first)], gy, b, first, last, gy_s, gy_r))

    for item in range(z_ring.items):
        z_ring.take(item)
        if item < y_ring.items:
            y_ring.take(item)
        t = (2 * item + 2) / X_PARTS - 1
        if t == 1:
            keep_j(1, xy[1])
            keep_j(NY - 1, xy[NY - 1])
        if t == 2:
            keep_j(2, xy[2])
            gram(0, 3)
            arrivals.append(scatter(gp, gr, 0, 0, 3, g_s, g_r))
        if t == 3:
            gram(3, 4)
            arrivals.append(scatter(gp, gr, 1, 3, 4, g_s, g_r))
        if t == 4:
            gram(4, 5)
            arrivals.append(scatter(gp, gr, 2, 4, 5, g_s, g_r))
        if t == 5:
            gram(5, 7)
            arrivals.append(scatter(gp, gr, 3, 5, 7, g_s, g_r))
            drain_g(0, (0, 1))
        if t == 6:
            gram(7, NZ)
            arrivals.append(scatter(gp, gr, 4, 7, NZ, g_s, g_r))
            drain_g(1, (2, 3))

    group = NY * sub

    def place(slot, pos):
        first = (order[pos] + 1) % NZ * group
        return pl.ds(pl.multiple_of(first + lax.rem(y - slot + NY, NY) * sub, sub), sub)

    def settle(b):
        first, last = y_spans[b]
        for pos in range(first, last):
            gj[place(0, pos), :] = gs[pos]
        y_waits[b]()
        for slot in range(1, NY):
            for pos in range(first, last):
                gj[place(slot, pos), :] = gy[slot - 1, pos]

    mine = pl.ds(pl.multiple_of(y * rows, rows), rows)
    lanes = owned * NY // 2
    near = [(0, 1, 1, 0, rows), (0, -1, NZ - 1, 0, rows)]
    last = [(2, 2, 4, 0, half), (NZ - 2, -2, 4, half, half)]
    t_moves = (
        near + [(1, 1, 2, 0, rows), (NZ - 1, -1, NZ - 2, 0, rows), (2, 1, 3, 0, rows), (NZ - 2, -1, NZ - 3, 0, rows)] + last,
        near + [(0, 2, 2, 0, rows), (0, -2, NZ - 2, 0, rows), (1, 2, 3, 0, rows), (NZ - 1, -2, NZ - 3, 0, rows)] + last,
    )

    def t_copy(part, k, src, dst):
        return copy(src, dst, tz_s.at[part], tz_r.at[part, k // 2], at_z(t_moves[part][k][1]))

    def t_start(part, first):
        for k in range(first, first + 2):
            source, _, slot, start, size = t_moves[part][k]
            own = tt.at[part, pl.ds(pl.multiple_of(y * rows + start, half), size)]
            src = tz.at[part, source, pl.ds(start, size)] if source else own
            t_copy(part, k, src, tz.at[part, slot, pl.ds(start, size)]).start()

    def t_wait(part, first):
        two = tz.at[part, pl.ds(0, 2 if first < 6 else 1)]
        t_copy(part, first, two, two).wait_recv()

    def t_open(part):
        tt[part] = gj[pl.ds(part * lanes, lanes), :].T
        t_start(part, 0)

    settle(0)
    t_open(0)
    drain_g(2, (4,))
    z_ring.close()
    t_wait(0, 0)
    t_start(0, 2)
    settle(1)
    settle(2)
    t_open(1)
    t_start(1, 2)
    t_wait(0, 2)
    t_start(0, 4)
    t_start(0, 6)

    right = split(gj[...])
    k_waits, arrivals = [], []

    def square(first, last):
        for pos in range(first, last):
            slot = order[pos]
            halves_t = [tz[part, slot] if pos else tt[part, mine, :] for part in range(2)]
            whole = jnp.concatenate(halves_t, axis=1)
            hi, lo = split(pltpu.roll(whole, slot * group, 1) if pos else whole)
            thi[span(pos, pos + 1), :] = hi
            tlo[span(pos, pos + 1), :] = lo
        where = span(first, last)
        block = dot3((thi[where, :], tlo[where, :]), right, 1, 0)
        cp[first:last] = block.reshape(last - first, rows, wide)

    def drain_c(first, last, which):
        for one in which:
            arrivals[one]()
        for pos in range(first, last):
            value = CUBIC_TERM * gs[pos] + QUINTIC_TERM * gathered(cp, cr, pos)
            if pos == 0:
                lane = lax.broadcasted_iota(jnp.int32, value.shape, 1)
                diagonal = lax.broadcasted_iota(jnp.int32, value.shape, 0) + (y * rows + col * sub)
                value = value + jnp.where(lane == diagonal, LINEAR_TERM, 0.0)
            pp[pos, x, core] = value

    first_span = pl.ds(0, spans[0][1])
    u_every = pp.at[first_span, pl.ds(0, nx - 1), core]
    u_all = copy(u_every, u_every, u_s, u_r, twin)
    v_mine, v_there = pp.at[first_span, :, core], pp.at[first_span, :, 1 - core]
    to_twin, from_twin = copy(v_mine, v_mine, v_s, v_r, twin), copy(v_there, v_there, v_s, v_r, twin)

    def to_chips():
        part = pp.at[first_span, x, core]
        for j in (2, 1, 3):
            copy(part, part, u_s, u_r, at_x(j)).start()

    def to_all(b, first, last):
        part = pp.at[pl.ds(first, last - first), x, core]
        every = pp.at[pl.ds(0, nc - 1), pl.ds(0, last - first), 0]
        return fan(nc, every, p_s.at[b], p_r.at[b], lambda j: (part, part, at_col(j)))

    old = closing[:]
    closing.clear()
    square(0, 1)
    arrivals.append(scatter(cp, cr, 0, 0, 1, c_s, c_r))
    y_ring.close()
    for done in old:
        done()
    for b in range(1, 3):
        t_wait(1, 2 * b - 2)
        t_start(1, 2 * b + 2)
        square(2 * b - 1, 2 * b + 1)
        arrivals.append(scatter(cp, cr, b, 2 * b - 1, 2 * b + 1, c_s, c_r))
    t_wait(0, 4)
    t_wait(1, 4)
    square(5, 7)
    arrivals.append(scatter(cp, cr, 3, 5, 7, c_s, c_r))
    t_wait(0, 6)
    t_wait(1, 6)
    square(7, NZ)
    arrivals.append(scatter(cp, cr, 4, 7, NZ, c_s, c_r))
    drain_c(0, 5, (0, 1, 2))
    to_chips()
    drain_c(5, 7, (3,))
    from_all = [to_all(0, 5, 7)]
    drain_c(7, NZ, (4,))
    from_all.append(to_all(1, 7, NZ))
    for b, (first, last) in enumerate(spans):
        k_waits.append(spread_y(pp.at[pl.ds(first, last - first), x, core], qy, b, first, last, qk_s, qk_r))
    u_all.wait_recv()
    to_twin.start()
    for half_t in range(2):
        every = tz.at[half_t, pl.ds(0, NZ - 1)]
        t_copy(half_t, 0, every, every).wait_send()

    cut = (width // 128 + 1) // 2 * 128
    parts = (pl.ds(0, cut), pl.ds(cut, width - cut))
    most = NZ // 2
    early = most * rows
    from_twin.wait_recv()
    known = jnp.concatenate([pp[:most].reshape(early, wide), jnp.zeros((NZ * rows - early, wide), F32)], axis=0)
    hi, lo = split(known.T)
    pthi[...] = hi
    ptlo[...] = lo
    for c in range(2):
        block = dot3((pthi[...], ptlo[...]), (xhi[:, parts[c]], xlo[:, parts[c]]), 1, 0)
        op[:, :, parts[c]] = block.reshape(NY, rows, block.shape[-1])
    from_all[0]()
    from_all[1]()
    late = split(pp[most:].reshape(NZ * rows - early, wide).T)

    def product(c):
        block = dot3(late, (xhi[early:, parts[c]], xlo[early:, parts[c]]), 1, 0)
        op[:, :, parts[c]] = op[:, :, parts[c]] + block.reshape(NY, rows, block.shape[-1])

    def pass_on(way, t, step, h, c):
        w = 0 if way > 0 else 1
        part = op.at[lax.rem(y + way * step + NY, NY), halves(h), parts[c]]
        copy(part, ry.at[w, t, :, parts[c]], ry_s.at[c], ry_r.at[min(t, 1), c], at_y(way)).start()

    def arrived(kind, c):
        here = ry.at[:, 1:3, :, parts[c]] if kind else ry.at[:, 0, :, parts[c]]
        copy(here, here, ry_s.at[c], ry_r.at[kind, c], at_y(1)).wait_recv()

    def begin(c):
        product(c)
        for way in (1, -1):
            pass_on(way, 0, 2, 0 if way > 0 else 1, c)
        for way in (1, -1):
            pass_on(way, 1, 1, 1 if way > 0 else 0, c)

    def finish(c):
        arrived(0, c)
        for way in (1, -1):
            w = h = 0 if way > 0 else 1
            to = lax.rem(y + way + NY, NY)
            op[to, halves(h), parts[c]] = op[to, halves(h), parts[c]] + ry[w, 0, :, parts[c]]
            pass_on(way, 2, 1, h, c)

    def squares_here():
        for pos in range(NZ):
            qk[place(0, pos), :] = pp[pos, x, core]
        for arrive in k_waits:
            arrive()
        for slot in range(1, NY):
            for pos in range(NZ):
                qk[place(slot, pos), :] = qy[slot - 1, pos]
        block = dot3((thi[...], tlo[...]), split(qk[...]), 1, 0)
        block = block * pp[...].reshape(NZ * rows, wide)
        columns = jnp.sum(block.reshape(NZ * rows // 8, 8, wide), axis=0)
        total = columns[:, :128]
        for c in range(1, wide // 128):
            total = total + columns[:, c * 128 : (c + 1) * 128]
        return total

    stages = ((nc, at_col, sqx, qx_s, qx_r), (NZ, at_z, sqz, qz_s, qz_r), (NY, at_y, sqy, qy_s, qy_r))

    def give(stage, total):
        n, device, buf, send_sem, recv_sem = stages[stage]
        sq[stage] = total
        return fan(n, buf, send_sem, recv_sem, lambda s: (sq.at[stage], buf.at[s - 1], device(s)))

    def take(stage, now, total):
        now()
        for one in range(stages[stage][0] - 1):
            total = total + stages[stage][2][one]
        return total

    begin(0)
    total = squares_here()
    now = give(0, total)
    begin(1)
    total = take(0, now, total)
    now = give(1, total)
    finish(0)
    finish(1)
    total = take(1, now, total)
    now = give(2, total)
    for done in closing[:-1]:
        done()
    total = take(2, now, total)
    squares = jnp.sum(jnp.sum(total, axis=1, keepdims=True), axis=0, keepdims=True)
    factor = TARGET_SCALE / jnp.sqrt(squares / (M * N) + EPSILON)

    u_all.wait_send()
    to_twin.wait_send()
    arrived(1, 0)
    arrived(1, 1)
    for h in range(2):
        total = op[y, halves(h), :] + (ry[0, 2 - h, :, :] + ry[1, 1 + h, :, :])
        out_ref[halves(h), :] = factor * total
    for c in range(2):
        every = ry.at[:, :, :, parts[c]]
        copy(every, every, ry_s.at[c], ry_r.at[0, c], at_y(1)).wait_send()
    closing[-1]()


def body(nc, iterate):
    rows, width = iterate.shape
    sub = rows // nc
    wide = NY * rows
    owned = NY * NZ * sub
    vmem = pltpu.VMEM
    dma = pltpu.SemaphoreType.DMA

    def pair(*shape):
        return [dma(shape), dma(shape)]

    return pl.pallas_call(
        functools.partial(kernel, nc),
        out_shape=vmem((rows, width), F32),
        in_specs=[pl.BlockSpec(memory_space=pl.ANY)],
        out_specs=pl.BlockSpec(memory_space=vmem),
        scratch_shapes=[
            vmem((rows, width), F32),
            vmem((NZ, rows, width), F32),
            vmem((NY, rows, width), F32),
            vmem((NZ * rows, width), BF16),
            vmem((NZ * rows, width), BF16),
            vmem((wide, width), BF16),
            vmem((wide, width), BF16),
            vmem((NZ, rows, wide), F32),
            vmem((nc - 1, NZ, sub, wide), F32),
            vmem((NZ, sub, wide), F32),
            vmem((NY - 1, NZ, sub, wide), F32),
            vmem((owned, wide), F32),
            vmem((2, wide, owned // 2), F32),
            vmem((2, NZ, rows, owned // 2), F32),
            vmem((NZ * rows, owned), BF16),
            vmem((NZ * rows, owned), BF16),
            vmem((NZ, rows, wide), F32),
            vmem((nc - 1, NZ, sub, wide), F32),
            vmem((NZ, nc // 2, 2, sub, wide), F32),
            vmem((NY - 1, NZ, sub, wide), F32),
            vmem((owned, wide), F32),
            vmem((wide, NZ * rows), BF16),
            vmem((wide, NZ * rows), BF16),
            vmem((NY, rows, width), F32),
            vmem((2, 3, rows // 2, width), F32),
            vmem((3, 8, 128), F32),
            vmem((nc - 1, 8, 128), F32),
            vmem((NZ - 1, 8, 128), F32),
            vmem((NY - 1, 8, 128), F32),
            dma,
        ]
        + [dma, dma((ring_items(NZ, X_PARTS),))]
        + [dma, dma((ring_items(NY, X_PARTS),))]
        + pair(5)
        + pair(3)
        + [dma((2,)), dma((2, 4))]
        + pair(5)
        + [dma] * 4
        + pair(2)
        + pair(2)
        + [dma((2,)), dma((2, 2))]
        + [dma] * 6,
        compiler_params=pltpu.CompilerParams(
            collective_id=0, has_side_effects=True, vmem_limit_bytes=56 * 1024 * 1024
        ),
    )(iterate)


def solution(mesh):
    return jax.shard_map(
        functools.partial(body, mesh.shape["col"]),
        mesh=mesh,
        in_specs=(P("row", "col"),),
        out_specs=P("row", "col"),
        check_vma=False,
    )
```

```python
import functools
import jax
import jax.numpy as jnp
from jax import lax
from jax.experimental import pallas as pl
from jax.experimental.pallas import tpu as pltpu
from jax.sharding import PartitionSpec as P

M = 2048
N = 7168
NY = 4
NZ = 8
X_PARTS = 4

LINEAR_TERM = 3.4445
CUBIC_TERM = -4.775
QUINTIC_TERM = 2.0315
TARGET_SCALE = 0.2
EPSILON = 1e-07
MESH = pl.DeviceIdType.MESH
F32 = jnp.float32
BF16 = jnp.bfloat16


def split(value):
    high = value.astype(BF16)
    return high, (value - high.astype(F32)).astype(BF16)


def dot3(left, right, left_dim, right_dim):
    return lax.dot_general(
        jnp.concatenate([left[0], left[0], left[1]], axis=left_dim),
        jnp.concatenate([right[0], right[1], right[0]], axis=right_dim),
        (((left_dim,), (right_dim,)), ((), ())),
        preferred_element_type=F32,
    )


class Ring:
    def __init__(self, n, parts, device, src, land, two, every, send_sem, recv_sem):
        self.parts, self.device, self.src, self.land = parts, device, src, land
        self.two, self.every, self.send_sem, self.recv_sem = two, every, send_sem, recv_sem
        self.items = ring_items(n, parts)

    def copy(self, src, dst, t, way):
        return pltpu.make_async_remote_copy(
            src_ref=src,
            dst_ref=dst,
            send_sem=self.send_sem,
            recv_sem=self.recv_sem.at[t],
            device_id=self.device(way),
            device_id_type=MESH,
        )

    def send(self, t):
        for way in (1, -1):
            d, h = t // self.parts, t % self.parts
            h = h if way > 0 else self.parts - 1 - h
            self.copy(self.src(way, d, h), self.land(way, d, h), t, way).start()

    def open(self):
        for t in range(min(self.parts, self.items)):
            self.send(t)

    def take(self, t):
        self.copy(self.two, self.two, t, 1).wait_recv()
        if t + self.parts < self.items:
            self.send(t + self.parts)

    def close(self):
        self.copy(self.every, self.every, 0, 1).wait_send()


def ring_items(n, parts):
    return parts * (n - 1) // 2


def slot_order(n):
    out = [0]
    for s in range(1, n // 2):
        out += [s, n - s]
    return out + [n // 2]


def kernel(
    nc, x_hbm, out_ref,
    xv, xz, xy, xhi, xlo, jhi, jlo, gp, gr, gs, gy, gj, tt, tz, thi, tlo, cp, cr, pp, qy, qk, pthi, ptlo, op, ry,
    sq, sqx, sqz, sqy,
    x_s, xz_s, xz_r, xy_s, xy_r, g_s, g_r, gy_s, gy_r, tz_s, tz_r, c_s, c_r, u_s, u_r, v_s, v_r, p_s, p_r, qk_s, qk_r, ry_s, ry_r,
    qx_s, qx_r, qz_s, qz_r, qy_s, qy_r,
):
    rows, width = xv.shape
    half = rows // 2
    sub = rows // nc
    owned = NZ * sub
    wide = NY * rows
    row, col = lax.axis_index("row"), lax.axis_index("col")
    y, z = lax.div(row, NZ), lax.rem(row, NZ)

    def at_y(step):
        return (lax.rem(y + step + NY, NY) * NZ + z, col)

    def at_z(step):
        return (y * NZ + lax.rem(z + step + NZ, NZ), col)

    nx = nc // 2
    x, core = lax.div(col, 2), lax.rem(col, 2)
    twin = (row, col + 1 - 2 * core)

    def at_x(step):
        return (row, lax.rem(x + step + nx, nx) * 2 + core)

    def at_col(step):
        return (row, lax.rem(col + step, nc))

    def copy(src, dst, send_sem, recv_sem, device):
        return pltpu.make_async_remote_copy(
            src_ref=src, dst_ref=dst, send_sem=send_sem, recv_sem=recv_sem, device_id=device, device_id_type=MESH
        )

    fetch = pltpu.make_async_copy(x_hbm, xv, x_s)
    fetch.start()
    barrier = pltpu.get_barrier_semaphore()
    friends = [at_z(1), at_z(-1), at_y(1), at_y(-1), at_y(2)]
    friends += [at_z(s) for s in range(2, NZ - 1)] + [at_col(s) for s in range(1, nc)]
    for friend in friends:
        pl.semaphore_signal(barrier, inc=1, device_id=friend, device_id_type=MESH)
    pl.semaphore_wait(barrier, len(friends))

    def halves(h):
        return pl.ds(h * half, half)

    def block_ring(n, parts, device, own, buf, send_sem, recv_sem):
        def src(way, d, h):
            return own(h) if d == 0 else buf.at[way * d % n, pl.ds(h * (rows // parts), rows // parts)]

        def land(way, d, h):
            return buf.at[way * (d + 1) % n, pl.ds(h * (rows // parts), rows // parts)]

        two = buf.at[0, pl.ds(0, 2 * (rows // parts))]
        return Ring(n, parts, device, src, land, two, buf.at[pl.ds(0, n - 1)], send_sem, recv_sem)

    def own_x(h):
        return x_hbm.at[pl.ds(h * (rows // X_PARTS), rows // X_PARTS)]

    z_ring = block_ring(NZ, X_PARTS, at_z, own_x, xz, xz_s, xz_r)
    y_ring = block_ring(NY, X_PARTS, at_y, own_x, xy, xy_s, xy_r)
    z_ring.open()
    y_ring.open()
    fetch.wait()
    order = slot_order(NZ)
    closing = []

    def span(first, last):
        return pl.ds(first * rows, (last - first) * rows)

    def keep_j(slot, value):
        where = pl.ds(pl.multiple_of(lax.rem(y - slot + NY, NY) * rows, rows), rows)
        hi, lo = split(value)
        jhi[where, :] = hi
        jlo[where, :] = lo

    def keep_i(pos, value):
        hi, lo = split(value)
        xhi[span(pos, pos + 1), :] = hi
        xlo[span(pos, pos + 1), :] = lo

    def each(n, act):
        for j in sorted(range(1, n), key=lambda j: -min(j, n - j)):
            act(j)

    def fan(n, whole, send_sem, recv_sem, make):
        every = copy(whole, whole, send_sem, recv_sem, twin)
        each(n, lambda j: copy(*make(j)[:2], send_sem, recv_sem, make(j)[2]).start())
        closing.append(every.wait_send)
        return every.wait_recv

    def scatter(part, buf, b, first, last, send_sem, recv_sem):
        def make(j):
            to = at_col(j)
            mine_there = pl.ds(pl.multiple_of(to[1] * sub, sub), sub)
            return part.at[pl.ds(first, last - first), mine_there], buf.at[j - 1, pl.ds(first, last - first)], to

        return fan(nc, buf.at[:, pl.ds(first, last - first)], send_sem.at[b], recv_sem.at[b], make)

    def gathered(part, buf, pos):
        total = part[pos, pl.ds(pl.multiple_of(col * sub, sub), sub), :]
        for j in range(1, nc):
            total = total + buf[j - 1, pos]
        return total

    def spread_y(src, buf, b, first, last, send_sem, recv_sem):
        where = pl.ds(first, last - first)
        return fan(
            NY, buf.at[:, where], send_sem.at[b], recv_sem.at[b], lambda s: (src, buf.at[s - 1, where], at_y(s))
        )

    keep_i(0, xv[...])
    keep_j(0, xv[...])
    y_waits, arrivals = [], []
    spans = ((0, 5), (5, NZ))

    def gram(first, last):
        for pos in range(first, last):
            if pos:
                keep_i(pos, xz[order[pos]])
        where = span(first, last)
        block = dot3((xhi[where, :], xlo[where, :]), (jhi[...], jlo[...]), 1, 1)
        gp[first:last] = block.reshape(last - first, rows, wide)

    y_spans = ((0, 4), (4, 7), (7, NZ))

    def drain_g(b, which):
        first, last = y_spans[b]
        for one in which:
            arrivals[one]()
        for pos in range(first, last):
            gs[pos] = gathered(gp, gr, pos)
        y_waits.append(spread_y(gs.at[pl.ds(first, last - first)], gy, b, first, last, gy_s, gy_r))

    for item in range(z_ring.items):
        z_ring.take(item)
        if item < y_ring.items:
            y_ring.take(item)
        t = (2 * item + 2) / X_PARTS - 1
        if t == 1:
            keep_j(1, xy[1])
            keep_j(NY - 1, xy[NY - 1])
        if t == 2:
            keep_j(2, xy[2])
            gram(0, 3)
            arrivals.append(scatter(gp, gr, 0, 0, 3, g_s, g_r))
        if t == 3:
            gram(3, 4)
            arrivals.append(scatter(gp, gr, 1, 3, 4, g_s, g_r))
        if t == 4:
            gram(4, 5)
            arrivals.append(scatter(gp, gr, 2, 4, 5, g_s, g_r))
            drain_g(0, (0, 1))
        if t == 5:
            gram(5, 7)
            arrivals.append(scatter(gp, gr, 3, 5, 7, g_s, g_r))
        if t == 6:
            gram(7, NZ)
            arrivals.append(scatter(gp, gr, 4, 7, NZ, g_s, g_r))

    group = NY * sub

    def place(slot, pos):
        first = (order[pos] + 1) % NZ * group
        return pl.ds(pl.multiple_of(first + lax.rem(y - slot + NY, NY) * sub, sub), sub)

    def settle(b):
        first, last = y_spans[b]
        for pos in range(first, last):
            gj[place(0, pos), :] = gs[pos]
        y_waits[b]()
        for slot in range(1, NY):
            for pos in range(first, last):
                gj[place(slot, pos), :] = gy[slot - 1, pos]

    pair_of_y, in_pair = lax.div(y, 2), lax.rem(y, 2)
    mine = pl.ds(pl.multiple_of(in_pair * rows, rows), rows)
    lanes = owned * NY // 2
    near = [(0, 1, 1, 0, rows), (0, -1, NZ - 1, 0, rows)]
    last = [(2, 2, 4, 0, half), (NZ - 2, -2, 4, half, half)]
    t_moves = (
        near + [(1, 1, 2, 0, rows), (NZ - 1, -1, NZ - 2, 0, rows), (2, 1, 3, 0, rows), (NZ - 2, -1, NZ - 3, 0, rows)] + last,
        near + [(0, 2, 2, 0, rows), (0, -2, NZ - 2, 0, rows), (1, 2, 3, 0, rows), (NZ - 1, -2, NZ - 3, 0, rows)] + last,
    )

    def t_copy(part, k, src, dst):
        return copy(src, dst, tz_s.at[part], tz_r.at[part, k // 2], at_z(t_moves[part][k][1]))

    def t_start(part, first):
        for k in range(first, first + 2):
            source, _, slot, start, size = t_moves[part][k]
            own = tt.at[part, pl.ds(pl.multiple_of(in_pair * rows + start, half), size)]
            src = tz.at[part, source, pl.ds(start, size)] if source else own
            t_copy(part, k, src, tz.at[part, slot, pl.ds(start, size)]).start()

    def t_wait(part, first):
        two = tz.at[part, pl.ds(0, 2 if first < 6 else 1)]
        t_copy(part, first, two, two).wait_recv()

    def t_open(part):
        columns = pl.ds(pl.multiple_of(pair_of_y * 2 * rows, 2 * rows), 2 * rows)
        tt[part] = gj[pl.ds(part * lanes, lanes), columns].T
        t_start(part, 0)

    settle(0)
    t_open(0)
    drain_g(1, (2, 3))
    drain_g(2, (4,))
    z_ring.close()
    t_wait(0, 0)
    t_start(0, 2)
    settle(1)
    settle(2)
    t_open(1)
    t_start(1, 2)
    t_wait(0, 2)
    t_start(0, 4)
    t_start(0, 6)

    right = split(gj[...])
    k_waits, arrivals = [], []

    def square(first, last):
        for pos in range(first, last):
            slot = order[pos]
            halves_t = [tz[part, slot] if pos else tt[part, mine, :] for part in range(2)]
            whole = jnp.concatenate(halves_t, axis=1)
            hi, lo = split(pltpu.roll(whole, slot * group, 1) if pos else whole)
            thi[span(pos, pos + 1), :] = hi
            tlo[span(pos, pos + 1), :] = lo
        where = span(first, last)
        block = dot3((thi[where, :], tlo[where, :]), right, 1, 0)
        cp[first:last] = block.reshape(last - first, rows, wide)

    def drain_c(first, last, which):
        for one in which:
            arrivals[one]()
        for pos in range(first, last):
            value = CUBIC_TERM * gs[pos] + QUINTIC_TERM * gathered(cp, cr, pos)
            if pos == 0:
                lane = lax.broadcasted_iota(jnp.int32, value.shape, 1)
                diagonal = lax.broadcasted_iota(jnp.int32, value.shape, 0) + (y * rows + col * sub)
                value = value + jnp.where(lane == diagonal, LINEAR_TERM, 0.0)
            pp[pos, x, core] = value

    first_span = pl.ds(0, spans[0][1])
    u_every = pp.at[first_span, pl.ds(0, nx - 1), core]
    u_all = copy(u_every, u_every, u_s, u_r, twin)
    v_mine, v_there = pp.at[first_span, :, core], pp.at[first_span, :, 1 - core]
    to_twin, from_twin = copy(v_mine, v_mine, v_s, v_r, twin), copy(v_there, v_there, v_s, v_r, twin)

    def to_chips():
        part = pp.at[first_span, x, core]
        for j in (2, 1, 3):
            copy(part, part, u_s, u_r, at_x(j)).start()

    def to_all(b, first, last):
        part = pp.at[pl.ds(first, last - first), x, core]
        every = pp.at[pl.ds(0, nc - 1), pl.ds(0, last - first), 0]
        return fan(nc, every, p_s.at[b], p_r.at[b], lambda j: (part, part, at_col(j)))

    old = closing[:]
    closing.clear()
    square(0, 1)
    arrivals.append(scatter(cp, cr, 0, 0, 1, c_s, c_r))
    y_ring.close()
    for done in old:
        done()
    for b in range(1, 3):
        t_wait(1, 2 * b - 2)
        t_start(1, 2 * b + 2)
        square(2 * b - 1, 2 * b + 1)
        arrivals.append(scatter(cp, cr, b, 2 * b - 1, 2 * b + 1, c_s, c_r))
    t_wait(0, 4)
    t_wait(1, 4)
    square(5, 7)
    arrivals.append(scatter(cp, cr, 3, 5, 7, c_s, c_r))
    t_wait(0, 6)
    t_wait(1, 6)
    square(7, NZ)
    arrivals.append(scatter(cp, cr, 4, 7, NZ, c_s, c_r))

    def rows_to_y(b, first, last):
        k_waits.append(spread_y(pp.at[pl.ds(first, last - first), x, core], qy, b, first, last, qk_s, qk_r))

    drain_c(0, 5, (0, 1, 2))
    to_chips()
    rows_to_y(0, 0, 5)
    drain_c(5, 7, (3,))
    from_all = [to_all(0, 5, 7)]
    drain_c(7, NZ, (4,))
    from_all.append(to_all(1, 7, NZ))
    rows_to_y(1, 5, 7)
    rows_to_y(2, 7, NZ)
    u_all.wait_recv()
    to_twin.start()
    for half_t in range(2):
        every = tz.at[half_t, pl.ds(0, NZ - 1)]
        t_copy(half_t, 0, every, every).wait_send()

    cut = width - 256
    parts = (pl.ds(0, cut), pl.ds(cut, width - cut))
    most = NZ // 2
    early = most * rows
    from_twin.wait_recv()
    known = jnp.concatenate([pp[:most].reshape(early, wide), jnp.zeros((NZ * rows - early, wide), F32)], axis=0)
    hi, lo = split(known.T)
    pthi[...] = hi
    ptlo[...] = lo
    for c in range(2):
        block = dot3((pthi[...], ptlo[...]), (xhi[:, parts[c]], xlo[:, parts[c]]), 1, 0)
        op[:, :, parts[c]] = block.reshape(NY, rows, block.shape[-1])
    from_all[0]()
    from_all[1]()
    late = split(pp[most:].reshape(NZ * rows - early, wide).T)

    def product(c):
        block = dot3(late, (xhi[early:, parts[c]], xlo[early:, parts[c]]), 1, 0)
        op[:, :, parts[c]] = op[:, :, parts[c]] + block.reshape(NY, rows, block.shape[-1])

    def pass_on(way, t, step, h, c):
        w = 0 if way > 0 else 1
        part = op.at[lax.rem(y + way * step + NY, NY), halves(h), parts[c]]
        copy(part, ry.at[w, t, :, parts[c]], ry_s.at[c], ry_r.at[min(t, 1), c], at_y(way)).start()

    def arrived(kind, c):
        here = ry.at[:, 1:3, :, parts[c]] if kind else ry.at[:, 0, :, parts[c]]
        copy(here, here, ry_s.at[c], ry_r.at[kind, c], at_y(1)).wait_recv()

    def begin(c):
        product(c)
        for way in (1, -1):
            pass_on(way, 0, 2, 0 if way > 0 else 1, c)
        for way in (1, -1):
            pass_on(way, 1, 1, 1 if way > 0 else 0, c)

    def finish(c):
        arrived(0, c)
        for way in (1, -1):
            w = h = 0 if way > 0 else 1
            to = lax.rem(y + way + NY, NY)
            op[to, halves(h), parts[c]] = op[to, halves(h), parts[c]] + ry[w, 0, :, parts[c]]
            pass_on(way, 2, 1, h, c)

    def squares_here():
        for pos in range(NZ):
            qk[place(0, pos), :] = pp[pos, x, core]
        for arrive in k_waits:
            arrive()
        for slot in range(1, NY):
            for pos in range(NZ):
                qk[place(slot, pos), :] = qy[slot - 1, pos]
        block = dot3((thi[...], tlo[...]), split(qk[...]), 1, 0)
        block = block * pp[...].reshape(NZ * rows, wide)
        columns = jnp.sum(block.reshape(NZ * rows // 8, 8, wide), axis=0)
        total = columns[:, :128]
        for c in range(1, wide // 128):
            total = total + columns[:, c * 128 : (c + 1) * 128]
        return total

    stages = ((nc, at_col, sqx, qx_s, qx_r), (NZ, at_z, sqz, qz_s, qz_r), (NY, at_y, sqy, qy_s, qy_r))

    def give(stage, total):
        n, device, buf, send_sem, recv_sem = stages[stage]
        sq[stage] = total
        return fan(n, buf, send_sem, recv_sem, lambda s: (sq.at[stage], buf.at[s - 1], device(s)))

    def take(stage, now, total):
        now()
        for one in range(stages[stage][0] - 1):
            total = total + stages[stage][2][one]
        return total

    begin(0)
    total = squares_here()
    now = give(0, total)
    begin(1)
    total = take(0, now, total)
    now = give(1, total)
    finish(0)
    finish(1)
    total = take(1, now, total)
    now = give(2, total)
    for done in closing[:-1]:
        done()
    total = take(2, now, total)
    squares = jnp.sum(jnp.sum(total, axis=1, keepdims=True), axis=0, keepdims=True)
    factor = TARGET_SCALE / jnp.sqrt(squares / (M * N) + EPSILON)

    u_all.wait_send()
    to_twin.wait_send()
    arrived(1, 0)
    arrived(1, 1)
    for h in range(2):
        total = op[y, halves(h), :] + (ry[0, 2 - h, :, :] + ry[1, 1 + h, :, :])
        out_ref[halves(h), :] = factor * total
    for c in range(2):
        every = ry.at[:, :, :, parts[c]]
        copy(every, every, ry_s.at[c], ry_r.at[0, c], at_y(1)).wait_send()
    closing[-1]()


def body(nc, iterate):
    rows, width = iterate.shape
    sub = rows // nc
    wide = NY * rows
    owned = NY * NZ * sub
    vmem = pltpu.VMEM
    dma = pltpu.SemaphoreType.DMA

    def pair(*shape):
        return [dma(shape), dma(shape)]

    return pl.pallas_call(
        functools.partial(kernel, nc),
        out_shape=vmem((rows, width), F32),
        in_specs=[pl.BlockSpec(memory_space=pl.ANY)],
        out_specs=pl.BlockSpec(memory_space=vmem),
        scratch_shapes=[
            vmem((rows, width), F32),
            vmem((NZ, rows, width), F32),
            vmem((NY, rows, width), F32),
            vmem((NZ * rows, width), BF16),
            vmem((NZ * rows, width), BF16),
            vmem((wide, width), BF16),
            vmem((wide, width), BF16),
            vmem((NZ, rows, wide), F32),
            vmem((nc - 1, NZ, sub, wide), F32),
            vmem((NZ, sub, wide), F32),
            vmem((NY - 1, NZ, sub, wide), F32),
            vmem((owned, wide), F32),
            vmem((2, 2 * rows, owned // 2), F32),
            vmem((2, NZ, rows, owned // 2), F32),
            vmem((NZ * rows, owned), BF16),
            vmem((NZ * rows, owned), BF16),
            vmem((NZ, rows, wide), F32),
            vmem((nc - 1, NZ, sub, wide), F32),
            vmem((NZ, nc // 2, 2, sub, wide), F32),
            vmem((NY - 1, NZ, sub, wide), F32),
            vmem((owned, wide), F32),
            vmem((wide, NZ * rows), BF16),
            vmem((wide, NZ * rows), BF16),
            vmem((NY, rows, width), F32),
            vmem((2, 3, rows // 2, width), F32),
            vmem((3, 8, 128), F32),
            vmem((nc - 1, 8, 128), F32),
            vmem((NZ - 1, 8, 128), F32),
            vmem((NY - 1, 8, 128), F32),
            dma,
        ]
        + [dma, dma((ring_items(NZ, X_PARTS),))]
        + [dma, dma((ring_items(NY, X_PARTS),))]
        + pair(5)
        + pair(3)
        + [dma((2,)), dma((2, 4))]
        + pair(5)
        + [dma] * 4
        + pair(2)
        + pair(3)
        + [dma((2,)), dma((2, 2))]
        + [dma] * 6,
        compiler_params=pltpu.CompilerParams(
            collective_id=0, has_side_effects=True, vmem_limit_bytes=56 * 1024 * 1024
        ),
    )(iterate)


def solution(mesh):
    return jax.shard_map(
        functools.partial(body, mesh.shape["col"]),
        mesh=mesh,
        in_specs=(P("row", "col"),),
        out_specs=P("row", "col"),
        check_vma=False,
    )
```

```python
import functools
import jax
import jax.numpy as jnp
from jax import lax
from jax.experimental import pallas as pl
from jax.experimental.pallas import tpu as pltpu
from jax.sharding import PartitionSpec as P

M = 2048
N = 7168
NY = 4
NZ = 8
X_PARTS = 4

LINEAR_TERM = 3.4445
CUBIC_TERM = -4.775
QUINTIC_TERM = 2.0315
TARGET_SCALE = 0.2
EPSILON = 1e-07
MESH = pl.DeviceIdType.MESH
F32 = jnp.float32
BF16 = jnp.bfloat16


def split(value):
    high = value.astype(BF16)
    return high, (value - high.astype(F32)).astype(BF16)


def dot3(left, right, left_dim, right_dim):
    return lax.dot_general(
        jnp.concatenate([left[0], left[0], left[1]], axis=left_dim),
        jnp.concatenate([right[0], right[1], right[0]], axis=right_dim),
        (((left_dim,), (right_dim,)), ((), ())),
        preferred_element_type=F32,
    )


class Ring:
    def __init__(self, n, parts, device, src, land, two, every, send_sem, recv_sem):
        self.parts, self.device, self.src, self.land = parts, device, src, land
        self.two, self.every, self.send_sem, self.recv_sem = two, every, send_sem, recv_sem
        self.items = ring_items(n, parts)

    def copy(self, src, dst, t, way):
        return pltpu.make_async_remote_copy(
            src_ref=src,
            dst_ref=dst,
            send_sem=self.send_sem,
            recv_sem=self.recv_sem.at[t],
            device_id=self.device(way),
            device_id_type=MESH,
        )

    def send(self, t):
        for way in (1, -1):
            d, h = t // self.parts, t % self.parts
            h = h if way > 0 else self.parts - 1 - h
            self.copy(self.src(way, d, h), self.land(way, d, h), t, way).start()

    def open(self):
        for t in range(min(self.parts, self.items)):
            self.send(t)

    def take(self, t):
        self.copy(self.two, self.two, t, 1).wait_recv()
        if t + self.parts < self.items:
            self.send(t + self.parts)

    def close(self):
        self.copy(self.every, self.every, 0, 1).wait_send()


def ring_items(n, parts):
    return parts * (n - 1) // 2


def slot_order(n):
    out = [0]
    for s in range(1, n // 2):
        out += [s, n - s]
    return out + [n // 2]


def kernel(
    nc, x_hbm, out_ref,
    xv, xz, xy, xhi, xlo, jhi, jlo, gp, gr, gs, gy, gj, tt, tz, thi, tlo, cp, cr, pp, qy, qk, pthi, ptlo, op, ry,
    sq, sqx, sqz, sqy,
    x_s, xz_s, xz_r, xy_s, xy_r, g_s, g_r, gy_s, gy_r, tz_s, tz_r, c_s, c_r, u_s, u_r, v_s, v_r, p_s, p_r, qk_s, qk_r, ry_s, ry_r,
    qx_s, qx_r, qz_s, qz_r, qy_s, qy_r,
):
    rows, width = xv.shape
    half = rows // 2
    sub = rows // nc
    owned = NZ * sub
    wide = NY * rows
    row, col = lax.axis_index("row"), lax.axis_index("col")
    y, z = lax.div(row, NZ), lax.rem(row, NZ)

    def at_y(step):
        return (lax.rem(y + step + NY, NY) * NZ + z, col)

    def at_z(step):
        return (y * NZ + lax.rem(z + step + NZ, NZ), col)

    nx = nc // 2
    x, core = lax.div(col, 2), lax.rem(col, 2)
    twin = (row, col + 1 - 2 * core)

    def at_x(step):
        return (row, lax.rem(x + step + nx, nx) * 2 + core)

    def at_col(step):
        return (row, lax.rem(col + step, nc))

    def copy(src, dst, send_sem, recv_sem, device):
        return pltpu.make_async_remote_copy(
            src_ref=src, dst_ref=dst, send_sem=send_sem, recv_sem=recv_sem, device_id=device, device_id_type=MESH
        )

    fetch = pltpu.make_async_copy(x_hbm, xv, x_s)
    fetch.start()
    barrier = pltpu.get_barrier_semaphore()
    friends = [at_z(1), at_z(-1), at_y(1), at_y(-1), at_y(2)]
    friends += [at_z(s) for s in range(2, NZ - 1)] + [at_col(s) for s in range(1, nc)]
    for friend in friends:
        pl.semaphore_signal(barrier, inc=1, device_id=friend, device_id_type=MESH)
    pl.semaphore_wait(barrier, len(friends))

    def halves(h):
        return pl.ds(h * half, half)

    def block_ring(n, parts, device, own, buf, send_sem, recv_sem):
        def src(way, d, h):
            return own(h) if d == 0 else buf.at[way * d % n, pl.ds(h * (rows // parts), rows // parts)]

        def land(way, d, h):
            return buf.at[way * (d + 1) % n, pl.ds(h * (rows // parts), rows // parts)]

        two = buf.at[0, pl.ds(0, 2 * (rows // parts))]
        return Ring(n, parts, device, src, land, two, buf.at[pl.ds(0, n - 1)], send_sem, recv_sem)

    def own_x(h):
        return x_hbm.at[pl.ds(h * (rows // X_PARTS), rows // X_PARTS)]

    z_ring = block_ring(NZ, X_PARTS, at_z, own_x, xz, xz_s, xz_r)
    y_ring = block_ring(NY, X_PARTS, at_y, own_x, xy, xy_s, xy_r)
    z_ring.open()
    y_ring.open()
    fetch.wait()
    order = slot_order(NZ)
    closing = []

    def span(first, last):
        return pl.ds(first * rows, (last - first) * rows)

    def keep_j(slot, value):
        where = pl.ds(pl.multiple_of(lax.rem(y - slot + NY, NY) * rows, rows), rows)
        hi, lo = split(value)
        jhi[where, :] = hi
        jlo[where, :] = lo

    def keep_i(pos, value):
        hi, lo = split(value)
        xhi[span(pos, pos + 1), :] = hi
        xlo[span(pos, pos + 1), :] = lo

    def each(n, act):
        for j in sorted(range(1, n), key=lambda j: -min(j, n - j)):
            act(j)

    def fan(n, whole, send_sem, recv_sem, make):
        every = copy(whole, whole, send_sem, recv_sem, twin)
        each(n, lambda j: copy(*make(j)[:2], send_sem, recv_sem, make(j)[2]).start())
        closing.append(every.wait_send)
        return every.wait_recv

    def scatter(part, buf, b, first, last, send_sem, recv_sem):
        def make(j):
            to = at_col(j)
            mine_there = pl.ds(pl.multiple_of(to[1] * sub, sub), sub)
            return part.at[pl.ds(first, last - first), mine_there], buf.at[j - 1, pl.ds(first, last - first)], to

        return fan(nc, buf.at[:, pl.ds(first, last - first)], send_sem.at[b], recv_sem.at[b], make)

    def gathered(part, buf, pos):
        total = part[pos, pl.ds(pl.multiple_of(col * sub, sub), sub), :]
        for j in range(1, nc):
            total = total + buf[j - 1, pos]
        return total

    def spread_y(src, buf, b, first, last, send_sem, recv_sem):
        where = pl.ds(first, last - first)
        return fan(
            NY, buf.at[:, where], send_sem.at[b], recv_sem.at[b], lambda s: (src, buf.at[s - 1, where], at_y(s))
        )

    keep_i(0, xv[...])
    keep_j(0, xv[...])
    y_waits, arrivals = [], []
    spans = ((0, 5), (5, NZ))

    def gram(first, last):
        for pos in range(first, last):
            if pos:
                keep_i(pos, xz[order[pos]])
        where = span(first, last)
        block = dot3((xhi[where, :], xlo[where, :]), (jhi[...], jlo[...]), 1, 1)
        gp[first:last] = block.reshape(last - first, rows, wide)

    y_spans = ((0, 4), (4, 7), (7, NZ))

    def drain_g(b, which):
        first, last = y_spans[b]
        for one in which:
            arrivals[one]()
        for pos in range(first, last):
            gs[pos] = gathered(gp, gr, pos)
        y_waits.append(spread_y(gs.at[pl.ds(first, last - first)], gy, b, first, last, gy_s, gy_r))

    for item in range(z_ring.items):
        z_ring.take(item)
        if item < y_ring.items:
            y_ring.take(item)
        t = (2 * item + 2) / X_PARTS - 1
        if t == 1:
            keep_j(1, xy[1])
            keep_j(NY - 1, xy[NY - 1])
        if t == 2:
            keep_j(2, xy[2])
            gram(0, 3)
            arrivals.append(scatter(gp, gr, 0, 0, 3, g_s, g_r))
        if t == 3:
            gram(3, 4)
            arrivals.append(scatter(gp, gr, 1, 3, 4, g_s, g_r))
        if t == 4:
            gram(4, 5)
            arrivals.append(scatter(gp, gr, 2, 4, 5, g_s, g_r))
            drain_g(0, (0, 1))
        if t == 5:
            gram(5, 7)
            arrivals.append(scatter(gp, gr, 3, 5, 7, g_s, g_r))
        if t == 6:
            gram(7, NZ)
            arrivals.append(scatter(gp, gr, 4, 7, NZ, g_s, g_r))

    group = NY * sub

    def place(slot, pos):
        first = (order[pos] + 1) % NZ * group
        return pl.ds(pl.multiple_of(first + lax.rem(y - slot + NY, NY) * sub, sub), sub)

    def settle(b):
        first, last = y_spans[b]
        for pos in range(first, last):
            gj[place(0, pos), :] = gs[pos]
        y_waits[b]()
        for slot in range(1, NY):
            for pos in range(first, last):
                gj[place(slot, pos), :] = gy[slot - 1, pos]

    pair_of_y, in_pair = lax.div(y, 2), lax.rem(y, 2)
    mine = pl.ds(pl.multiple_of(in_pair * rows, rows), rows)
    lanes = owned * NY // 2
    near = [(0, 1, 1, 0, rows), (0, -1, NZ - 1, 0, rows)]
    last = [(2, 2, 4, 0, half), (NZ - 2, -2, 4, half, half)]
    t_moves = (
        near + [(1, 1, 2, 0, rows), (NZ - 1, -1, NZ - 2, 0, rows), (2, 1, 3, 0, rows), (NZ - 2, -1, NZ - 3, 0, rows)] + last,
        near + [(0, 2, 2, 0, rows), (0, -2, NZ - 2, 0, rows), (2, 1, 3, 0, rows), (NZ - 2, -1, NZ - 3, 0, rows)] + last,
    )

    def t_copy(part, k, src, dst):
        return copy(src, dst, tz_s.at[part], tz_r.at[part, k // 2], at_z(t_moves[part][k][1]))

    def t_start(part, first):
        for k in range(first, first + 2):
            source, _, slot, start, size = t_moves[part][k]
            own = tt.at[part, pl.ds(pl.multiple_of(in_pair * rows + start, half), size)]
            src = tz.at[part, source, pl.ds(start, size)] if source else own
            t_copy(part, k, src, tz.at[part, slot, pl.ds(start, size)]).start()

    def t_wait(part, first):
        two = tz.at[part, pl.ds(0, 2 if first < 6 else 1)]
        t_copy(part, first, two, two).wait_recv()

    def t_open(part):
        columns = pl.ds(pl.multiple_of(pair_of_y * 2 * rows, 2 * rows), 2 * rows)
        tt[part] = gj[pl.ds(part * lanes, lanes), columns].T
        t_start(part, 0)

    settle(0)
    t_open(0)
    drain_g(1, (2, 3))
    drain_g(2, (4,))
    z_ring.close()
    t_wait(0, 0)
    t_start(0, 2)
    settle(1)
    settle(2)
    t_open(1)
    t_start(1, 2)
    t_wait(0, 2)
    t_start(0, 4)
    t_start(0, 6)

    right = split(gj[...])
    k_waits, arrivals = [], []

    def square(first, last):
        for pos in range(first, last):
            slot = order[pos]
            halves_t = [tz[part, slot] if pos else tt[part, mine, :] for part in range(2)]
            whole = jnp.concatenate(halves_t, axis=1)
            hi, lo = split(pltpu.roll(whole, slot * group, 1) if pos else whole)
            thi[span(pos, pos + 1), :] = hi
            tlo[span(pos, pos + 1), :] = lo
        where = span(first, last)
        block = dot3((thi[where, :], tlo[where, :]), right, 1, 0)
        cp[first:last] = block.reshape(last - first, rows, wide)

    def drain_c(first, last, which):
        for one in which:
            arrivals[one]()
        for pos in range(first, last):
            value = CUBIC_TERM * gs[pos] + QUINTIC_TERM * gathered(cp, cr, pos)
            if pos == 0:
                lane = lax.broadcasted_iota(jnp.int32, value.shape, 1)
                diagonal = lax.broadcasted_iota(jnp.int32, value.shape, 0) + (y * rows + col * sub)
                value = value + jnp.where(lane == diagonal, LINEAR_TERM, 0.0)
            pp[pos, x, core] = value

    first_span = pl.ds(0, spans[0][1])
    u_every = pp.at[first_span, pl.ds(0, nx - 1), core]
    u_all = copy(u_every, u_every, u_s, u_r, twin)
    v_mine, v_there = pp.at[first_span, :, core], pp.at[first_span, :, 1 - core]
    to_twin, from_twin = copy(v_mine, v_mine, v_s, v_r, twin), copy(v_there, v_there, v_s, v_r, twin)

    def to_chips():
        part = pp.at[first_span, x, core]
        for j in (2, 1, 3):
            copy(part, part, u_s, u_r, at_x(j)).start()

    def to_all(b, first, last):
        part = pp.at[pl.ds(first, last - first), x, core]
        every = pp.at[pl.ds(0, nc - 1), pl.ds(0, last - first), 0]
        return fan(nc, every, p_s.at[b], p_r.at[b], lambda j: (part, part, at_col(j)))

    old = closing[:]
    closing.clear()
    square(0, 1)
    arrivals.append(scatter(cp, cr, 0, 0, 1, c_s, c_r))
    y_ring.close()
    for done in old:
        done()
    t_wait(1, 0)
    t_wait(1, 2)
    t_start(1, 4)
    t_start(1, 6)
    for b in range(1, 3):
        square(2 * b - 1, 2 * b + 1)
        arrivals.append(scatter(cp, cr, b, 2 * b - 1, 2 * b + 1, c_s, c_r))
    t_wait(0, 4)
    t_wait(1, 4)
    square(5, 7)
    arrivals.append(scatter(cp, cr, 3, 5, 7, c_s, c_r))
    t_wait(0, 6)
    t_wait(1, 6)
    square(7, NZ)
    arrivals.append(scatter(cp, cr, 4, 7, NZ, c_s, c_r))

    def rows_to_y(b, first, last):
        k_waits.append(spread_y(pp.at[pl.ds(first, last - first), x, core], qy, b, first, last, qk_s, qk_r))

    drain_c(0, 5, (0, 1, 2))
    to_chips()
    rows_to_y(0, 0, 5)
    drain_c(5, 7, (3,))
    from_all = [to_all(0, 5, 7)]
    rows_to_y(1, 5, 7)
    drain_c(7, NZ, (4,))
    from_all.append(to_all(1, 7, NZ))
    rows_to_y(2, 7, NZ)
    u_all.wait_recv()
    to_twin.start()
    for half_t in range(2):
        every = tz.at[half_t, pl.ds(0, NZ - 1)]
        t_copy(half_t, 0, every, every).wait_send()

    cut = width - 256
    parts = (pl.ds(0, cut), pl.ds(cut, width - cut))
    most = NZ // 2
    early = most * rows
    from_twin.wait_recv()
    known = jnp.concatenate([pp[:most].reshape(early, wide), jnp.zeros((NZ * rows - early, wide), F32)], axis=0)
    hi, lo = split(known.T)
    pthi[...] = hi
    ptlo[...] = lo
    for c in range(2):
        block = dot3((pthi[...], ptlo[...]), (xhi[:, parts[c]], xlo[:, parts[c]]), 1, 0)
        op[:, :, parts[c]] = block.reshape(NY, rows, block.shape[-1])
    from_all[0]()
    from_all[1]()
    late = split(pp[most:].reshape(NZ * rows - early, wide).T)

    def product(c):
        block = dot3(late, (xhi[early:, parts[c]], xlo[early:, parts[c]]), 1, 0)
        op[:, :, parts[c]] = op[:, :, parts[c]] + block.reshape(NY, rows, block.shape[-1])

    def pass_on(way, t, step, h, c):
        w = 0 if way > 0 else 1
        part = op.at[lax.rem(y + way * step + NY, NY), halves(h), parts[c]]
        copy(part, ry.at[w, t, :, parts[c]], ry_s.at[c], ry_r.at[min(t, 1), c], at_y(way)).start()

    def arrived(kind, c):
        here = ry.at[:, 1:3, :, parts[c]] if kind else ry.at[:, 0, :, parts[c]]
        copy(here, here, ry_s.at[c], ry_r.at[kind, c], at_y(1)).wait_recv()

    def begin(c):
        product(c)
        for way in (1, -1):
            pass_on(way, 0, 2, 0 if way > 0 else 1, c)
        for way in (1, -1):
            pass_on(way, 1, 1, 1 if way > 0 else 0, c)

    def finish(c):
        arrived(0, c)
        for way in (1, -1):
            w = h = 0 if way > 0 else 1
            to = lax.rem(y + way + NY, NY)
            op[to, halves(h), parts[c]] = op[to, halves(h), parts[c]] + ry[w, 0, :, parts[c]]
            pass_on(way, 2, 1, h, c)

    def squares_here():
        for pos in range(NZ):
            qk[place(0, pos), :] = pp[pos, x, core]
        for arrive in k_waits:
            arrive()
        for slot in range(1, NY):
            for pos in range(NZ):
                qk[place(slot, pos), :] = qy[slot - 1, pos]
        block = dot3((thi[...], tlo[...]), split(qk[...]), 1, 0)
        block = block * pp[...].reshape(NZ * rows, wide)
        columns = jnp.sum(block.reshape(NZ * rows // 8, 8, wide), axis=0)
        total = columns[:, :128]
        for c in range(1, wide // 128):
            total = total + columns[:, c * 128 : (c + 1) * 128]
        return total

    stages = ((nc, at_col, sqx, qx_s, qx_r), (NZ, at_z, sqz, qz_s, qz_r), (NY, at_y, sqy, qy_s, qy_r))

    def give(stage, total):
        n, device, buf, send_sem, recv_sem = stages[stage]
        sq[stage] = total
        return fan(n, buf, send_sem, recv_sem, lambda s: (sq.at[stage], buf.at[s - 1], device(s)))

    def take(stage, now, total):
        now()
        for one in range(stages[stage][0] - 1):
            total = total + stages[stage][2][one]
        return total

    begin(0)
    total = squares_here()
    now = give(0, total)
    begin(1)
    total = take(0, now, total)
    now = give(1, total)
    finish(0)
    finish(1)
    total = take(1, now, total)
    now = give(2, total)
    for done in closing[:-1]:
        done()
    total = take(2, now, total)
    squares = jnp.sum(jnp.sum(total, axis=1, keepdims=True), axis=0, keepdims=True)
    factor = TARGET_SCALE / jnp.sqrt(squares / (M * N) + EPSILON)

    u_all.wait_send()
    to_twin.wait_send()
    arrived(1, 0)
    arrived(1, 1)
    for h in range(2):
        total = op[y, halves(h), :] + (ry[0, 2 - h, :, :] + ry[1, 1 + h, :, :])
        out_ref[halves(h), :] = factor * total
    for c in range(2):
        every = ry.at[:, :, :, parts[c]]
        copy(every, every, ry_s.at[c], ry_r.at[0, c], at_y(1)).wait_send()
    closing[-1]()


def body(nc, iterate):
    rows, width = iterate.shape
    sub = rows // nc
    wide = NY * rows
    owned = NY * NZ * sub
    vmem = pltpu.VMEM
    dma = pltpu.SemaphoreType.DMA

    def pair(*shape):
        return [dma(shape), dma(shape)]

    return pl.pallas_call(
        functools.partial(kernel, nc),
        out_shape=vmem((rows, width), F32),
        in_specs=[pl.BlockSpec(memory_space=pl.ANY)],
        out_specs=pl.BlockSpec(memory_space=vmem),
        scratch_shapes=[
            vmem((rows, width), F32),
            vmem((NZ, rows, width), F32),
            vmem((NY, rows, width), F32),
            vmem((NZ * rows, width), BF16),
            vmem((NZ * rows, width), BF16),
            vmem((wide, width), BF16),
            vmem((wide, width), BF16),
            vmem((NZ, rows, wide), F32),
            vmem((nc - 1, NZ, sub, wide), F32),
            vmem((NZ, sub, wide), F32),
            vmem((NY - 1, NZ, sub, wide), F32),
            vmem((owned, wide), F32),
            vmem((2, 2 * rows, owned // 2), F32),
            vmem((2, NZ, rows, owned // 2), F32),
            vmem((NZ * rows, owned), BF16),
            vmem((NZ * rows, owned), BF16),
            vmem((NZ, rows, wide), F32),
            vmem((nc - 1, NZ, sub, wide), F32),
            vmem((NZ, nc // 2, 2, sub, wide), F32),
            vmem((NY - 1, NZ, sub, wide), F32),
            vmem((owned, wide), F32),
            vmem((wide, NZ * rows), BF16),
            vmem((wide, NZ * rows), BF16),
            vmem((NY, rows, width), F32),
            vmem((2, 3, rows // 2, width), F32),
            vmem((3, 8, 128), F32),
            vmem((nc - 1, 8, 128), F32),
            vmem((NZ - 1, 8, 128), F32),
            vmem((NY - 1, 8, 128), F32),
            dma,
        ]
        + [dma, dma((ring_items(NZ, X_PARTS),))]
        + [dma, dma((ring_items(NY, X_PARTS),))]
        + pair(5)
        + pair(3)
        + [dma((2,)), dma((2, 4))]
        + pair(5)
        + [dma] * 4
        + pair(2)
        + pair(3)
        + [dma((2,)), dma((2, 2))]
        + [dma] * 6,
        compiler_params=pltpu.CompilerParams(
            collective_id=0, has_side_effects=True, vmem_limit_bytes=56 * 1024 * 1024
        ),
    )(iterate)


def solution(mesh):
    return jax.shard_map(
        functools.partial(body, mesh.shape["col"]),
        mesh=mesh,
        in_specs=(P("row", "col"),),
        out_specs=P("row", "col"),
        check_vma=False,
    )
```

```python
import functools
import jax
import jax.numpy as jnp
from jax import lax
from jax.experimental import pallas as pl
from jax.experimental.pallas import tpu as pltpu
from jax.sharding import PartitionSpec as P

M = 2048
N = 7168
NY = 4
NZ = 8
X_PARTS = 4

LINEAR_TERM = 3.4445
CUBIC_TERM = -4.775
QUINTIC_TERM = 2.0315
TARGET_SCALE = 0.2
EPSILON = 1e-07
MESH = pl.DeviceIdType.MESH
F32 = jnp.float32
BF16 = jnp.bfloat16


def split(value):
    high = value.astype(BF16)
    return high, (value - high.astype(F32)).astype(BF16)


def dot3(left, right, left_dim, right_dim):
    return lax.dot_general(
        jnp.concatenate([left[0], left[0], left[1]], axis=left_dim),
        jnp.concatenate([right[0], right[1], right[0]], axis=right_dim),
        (((left_dim,), (right_dim,)), ((), ())),
        preferred_element_type=F32,
    )


class Ring:
    def __init__(self, n, parts, device, src, land, two, every, send_sem, recv_sem):
        self.parts, self.device, self.src, self.land = parts, device, src, land
        self.two, self.every, self.send_sem, self.recv_sem = two, every, send_sem, recv_sem
        self.items = ring_items(n, parts)

    def copy(self, src, dst, t, way):
        return pltpu.make_async_remote_copy(
            src_ref=src,
            dst_ref=dst,
            send_sem=self.send_sem,
            recv_sem=self.recv_sem.at[t],
            device_id=self.device(way),
            device_id_type=MESH,
        )

    def send(self, t):
        for way in (1, -1):
            d, h = t // self.parts, t % self.parts
            h = h if way > 0 else self.parts - 1 - h
            self.copy(self.src(way, d, h), self.land(way, d, h), t, way).start()

    def open(self):
        for t in range(min(self.parts, self.items)):
            self.send(t)

    def take(self, t):
        self.copy(self.two, self.two, t, 1).wait_recv()
        if t + self.parts < self.items:
            self.send(t + self.parts)

    def close(self):
        self.copy(self.every, self.every, 0, 1).wait_send()


def ring_items(n, parts):
    return parts * (n - 1) // 2


def slot_order(n):
    out = [0]
    for s in range(1, n // 2):
        out += [s, n - s]
    return out + [n // 2]


def kernel(
    nc, x_hbm, out_ref,
    xv, xz, xy, xhi, xlo, jhi, jlo, gp, gr, gs, gy, gj, tt, tz, thi, tlo, cp, cr, pp, qy, qk, wq, pthi, ptlo, op, ry,
    sq, sqx, sqz, sqy,
    x_s, xz_s, xz_r, xy_s, xy_r, g_s, g_r, gy_s, gy_r, tz_s, tz_r, c_s, c_r, u_s, u_r, v_s, v_r, p_s, p_r, qk_s, qk_r, ry_s, ry_r,
    qx_s, qx_r, qz_s, qz_r, qy_s, qy_r,
):
    rows, width = xv.shape
    half = rows // 2
    sub = rows // nc
    owned = NZ * sub
    wide = NY * rows
    row, col = lax.axis_index("row"), lax.axis_index("col")
    y, z = lax.div(row, NZ), lax.rem(row, NZ)

    def at_y(step):
        return (lax.rem(y + step + NY, NY) * NZ + z, col)

    def at_z(step):
        return (y * NZ + lax.rem(z + step + NZ, NZ), col)

    nx = nc // 2
    x, core = lax.div(col, 2), lax.rem(col, 2)
    twin = (row, col + 1 - 2 * core)

    def at_x(step):
        return (row, lax.rem(x + step + nx, nx) * 2 + core)

    def at_col(step):
        return (row, lax.rem(col + step, nc))

    def copy(src, dst, send_sem, recv_sem, device):
        return pltpu.make_async_remote_copy(
            src_ref=src, dst_ref=dst, send_sem=send_sem, recv_sem=recv_sem, device_id=device, device_id_type=MESH
        )

    fetch = pltpu.make_async_copy(x_hbm, xv, x_s)
    fetch.start()
    barrier = pltpu.get_barrier_semaphore()
    friends = [at_z(1), at_z(-1), at_y(1), at_y(-1), at_y(2)]
    friends += [at_z(s) for s in range(2, NZ - 1)] + [at_col(s) for s in range(1, nc)]
    for friend in friends:
        pl.semaphore_signal(barrier, inc=1, device_id=friend, device_id_type=MESH)
    pl.semaphore_wait(barrier, len(friends))

    def halves(h):
        return pl.ds(h * half, half)

    def block_ring(n, parts, device, own, buf, send_sem, recv_sem):
        def src(way, d, h):
            return own(h) if d == 0 else buf.at[way * d % n, pl.ds(h * (rows // parts), rows // parts)]

        def land(way, d, h):
            return buf.at[way * (d + 1) % n, pl.ds(h * (rows // parts), rows // parts)]

        two = buf.at[0, pl.ds(0, 2 * (rows // parts))]
        return Ring(n, parts, device, src, land, two, buf.at[pl.ds(0, n - 1)], send_sem, recv_sem)

    def own_x(h):
        return x_hbm.at[pl.ds(h * (rows // X_PARTS), rows // X_PARTS)]

    z_ring = block_ring(NZ, X_PARTS, at_z, own_x, xz, xz_s, xz_r)
    y_ring = block_ring(NY, X_PARTS, at_y, own_x, xy, xy_s, xy_r)
    z_ring.open()
    y_ring.open()
    fetch.wait()
    order = slot_order(NZ)
    closing = []

    def span(first, last):
        return pl.ds(first * rows, (last - first) * rows)

    def keep_j(slot, value):
        where = pl.ds(pl.multiple_of(lax.rem(y - slot + NY, NY) * rows, rows), rows)
        hi, lo = split(value)
        jhi[where, :] = hi
        jlo[where, :] = lo

    def keep_i(pos, value):
        hi, lo = split(value)
        xhi[span(pos, pos + 1), :] = hi
        xlo[span(pos, pos + 1), :] = lo

    def each(n, act):
        for j in sorted(range(1, n), key=lambda j: -min(j, n - j)):
            act(j)

    def fan(n, whole, send_sem, recv_sem, make):
        every = copy(whole, whole, send_sem, recv_sem, twin)
        each(n, lambda j: copy(*make(j)[:2], send_sem, recv_sem, make(j)[2]).start())
        closing.append(every.wait_send)
        return every.wait_recv

    def scatter(part, buf, b, first, last, send_sem, recv_sem):
        def make(j):
            to = at_col(j)
            mine_there = pl.ds(pl.multiple_of(to[1] * sub, sub), sub)
            return part.at[pl.ds(first, last - first), mine_there], buf.at[j - 1, pl.ds(first, last - first)], to

        return fan(nc, buf.at[:, pl.ds(first, last - first)], send_sem.at[b], recv_sem.at[b], make)

    def gathered(part, buf, pos):
        total = part[pos, pl.ds(pl.multiple_of(col * sub, sub), sub), :]
        for j in range(1, nc):
            total = total + buf[j - 1, pos]
        return total

    def spread_y(src, buf, b, first, last, send_sem, recv_sem):
        where = pl.ds(first, last - first)
        return fan(
            NY, buf.at[:, where], send_sem.at[b], recv_sem.at[b], lambda s: (src, buf.at[s - 1, where], at_y(s))
        )

    keep_i(0, xv[...])
    keep_j(0, xv[...])
    y_waits, arrivals = [], []
    spans = ((0, 5), (5, NZ))

    def gram(first, last):
        for pos in range(first, last):
            if pos:
                keep_i(pos, xz[order[pos]])
        where = span(first, last)
        block = dot3((xhi[where, :], xlo[where, :]), (jhi[...], jlo[...]), 1, 1)
        gp[first:last] = block.reshape(last - first, rows, wide)

    y_spans = ((0, 4), (4, 7), (7, NZ))

    def drain_g(b, which):
        first, last = y_spans[b]
        for one in which:
            arrivals[one]()
        for pos in range(first, last):
            gs[pos] = gathered(gp, gr, pos)
        y_waits.append(spread_y(gs.at[pl.ds(first, last - first)], gy, b, first, last, gy_s, gy_r))

    for item in range(z_ring.items):
        z_ring.take(item)
        if item < y_ring.items:
            y_ring.take(item)
        t = (2 * item + 2) / X_PARTS - 1
        if t == 1:
            keep_j(1, xy[1])
            keep_j(NY - 1, xy[NY - 1])
        if t == 2:
            keep_j(2, xy[2])
            gram(0, 3)
            arrivals.append(scatter(gp, gr, 0, 0, 3, g_s, g_r))
        if t == 3:
            gram(3, 4)
            arrivals.append(scatter(gp, gr, 1, 3, 4, g_s, g_r))
        if t == 4:
            gram(4, 5)
            arrivals.append(scatter(gp, gr, 2, 4, 5, g_s, g_r))
            drain_g(0, (0, 1))
        if t == 5:
            gram(5, 7)
            arrivals.append(scatter(gp, gr, 3, 5, 7, g_s, g_r))
        if t == 6:
            gram(7, NZ)
            arrivals.append(scatter(gp, gr, 4, 7, NZ, g_s, g_r))

    group = NY * sub

    def place(slot, pos):
        first = (order[pos] + 1) % NZ * group
        return pl.ds(pl.multiple_of(first + lax.rem(y - slot + NY, NY) * sub, sub), sub)

    def settle(b):
        first, last = y_spans[b]
        for pos in range(first, last):
            gj[place(0, pos), :] = gs[pos]
        y_waits[b]()
        for slot in range(1, NY):
            for pos in range(first, last):
                gj[place(slot, pos), :] = gy[slot - 1, pos]

    pair_of_y, in_pair = lax.div(y, 2), lax.rem(y, 2)
    mine = pl.ds(pl.multiple_of(in_pair * rows, rows), rows)
    lanes = owned * NY // 2
    near = [(0, 1, 1, 0, rows), (0, -1, NZ - 1, 0, rows)]
    last = [(2, 2, 4, 0, half), (NZ - 2, -2, 4, half, half)]
    t_moves = (
        near + [(1, 1, 2, 0, rows), (NZ - 1, -1, NZ - 2, 0, rows), (2, 1, 3, 0, rows), (NZ - 2, -1, NZ - 3, 0, rows)] + last,
        near + [(0, 2, 2, 0, rows), (0, -2, NZ - 2, 0, rows), (2, 1, 3, 0, rows), (NZ - 2, -1, NZ - 3, 0, rows)] + last,
    )

    def t_copy(part, k, src, dst):
        return copy(src, dst, tz_s.at[part], tz_r.at[part, k // 2], at_z(t_moves[part][k][1]))

    def t_start(part, first):
        for k in range(first, first + 2):
            source, _, slot, start, size = t_moves[part][k]
            own = tt.at[part, pl.ds(pl.multiple_of(in_pair * rows + start, half), size)]
            src = tz.at[part, source, pl.ds(start, size)] if source else own
            t_copy(part, k, src, tz.at[part, slot, pl.ds(start, size)]).start()

    def t_wait(part, first):
        two = tz.at[part, pl.ds(0, 2 if first < 6 else 1)]
        t_copy(part, first, two, two).wait_recv()

    def t_open(part):
        columns = pl.ds(pl.multiple_of(pair_of_y * 2 * rows, 2 * rows), 2 * rows)
        tt[part] = gj[pl.ds(part * lanes, lanes), columns].T
        t_start(part, 0)

    settle(0)
    t_open(0)
    drain_g(1, (2, 3))
    drain_g(2, (4,))
    z_ring.close()
    t_wait(0, 0)
    t_start(0, 2)
    settle(1)
    settle(2)
    t_open(1)
    t_start(1, 2)
    t_wait(0, 2)
    t_start(0, 4)
    t_start(0, 6)

    right = split(gj[...])
    k_waits, arrivals = [], []

    def square(first, last):
        for pos in range(first, last):
            slot = order[pos]
            halves_t = [tz[part, slot] if pos else tt[part, mine, :] for part in range(2)]
            whole = jnp.concatenate(halves_t, axis=1)
            hi, lo = split(pltpu.roll(whole, slot * group, 1) if pos else whole)
            thi[span(pos, pos + 1), :] = hi
            tlo[span(pos, pos + 1), :] = lo
        where = span(first, last)
        block = dot3((thi[where, :], tlo[where, :]), right, 1, 0)
        cp[first:last] = block.reshape(last - first, rows, wide)

    def drain_c(first, last, which):
        for one in which:
            arrivals[one]()
        for pos in range(first, last):
            value = CUBIC_TERM * gs[pos] + QUINTIC_TERM * gathered(cp, cr, pos)
            if pos == 0:
                lane = lax.broadcasted_iota(jnp.int32, value.shape, 1)
                diagonal = lax.broadcasted_iota(jnp.int32, value.shape, 0) + (y * rows + col * sub)
                value = value + jnp.where(lane == diagonal, LINEAR_TERM, 0.0)
            pp[pos, x, core] = value

    first_span = pl.ds(0, spans[0][1])
    u_every = pp.at[first_span, pl.ds(0, nx - 1), core]
    u_all = copy(u_every, u_every, u_s, u_r, twin)
    v_mine, v_there = pp.at[first_span, :, core], pp.at[first_span, :, 1 - core]
    to_twin, from_twin = copy(v_mine, v_mine, v_s, v_r, twin), copy(v_there, v_there, v_s, v_r, twin)

    def to_chips():
        part = pp.at[first_span, x, core]
        for j in (2, 1, 3):
            copy(part, part, u_s, u_r, at_x(j)).start()

    def to_all(b, first, last):
        part = pp.at[pl.ds(first, last - first), x, core]
        every = pp.at[pl.ds(0, nc - 1), pl.ds(0, last - first), 0]
        return fan(nc, every, p_s.at[b], p_r.at[b], lambda j: (part, part, at_col(j)))

    old = closing[:]
    closing.clear()
    square(0, 1)
    arrivals.append(scatter(cp, cr, 0, 0, 1, c_s, c_r))
    y_ring.close()
    for done in old:
        done()
    t_wait(1, 0)
    t_wait(1, 2)
    t_start(1, 4)
    t_start(1, 6)
    for b in range(1, 3):
        square(2 * b - 1, 2 * b + 1)
        arrivals.append(scatter(cp, cr, b, 2 * b - 1, 2 * b + 1, c_s, c_r))
    t_wait(0, 4)
    t_wait(1, 4)
    square(5, 7)
    arrivals.append(scatter(cp, cr, 3, 5, 7, c_s, c_r))
    t_wait(0, 6)
    t_wait(1, 6)
    square(7, NZ)
    arrivals.append(scatter(cp, cr, 4, 7, NZ, c_s, c_r))

    def rows_to_y(b, first, last):
        k_waits.append(spread_y(pp.at[pl.ds(first, last - first), x, core], qy, b, first, last, qk_s, qk_r))

    drain_c(0, 5, (0, 1, 2))
    to_chips()
    rows_to_y(0, 0, 5)
    drain_c(5, 7, (3,))
    from_all = [to_all(0, 5, 7)]
    rows_to_y(1, 5, 7)
    drain_c(7, NZ, (4,))
    from_all.append(to_all(1, 7, NZ))
    rows_to_y(2, 7, NZ)

    def gather_q(part):
        blocks = range(4 * part, 4 * part + 4)
        for pos in blocks:
            qk[place(0, pos), :] = pp[pos, x, core]
        for arrive in k_waits[1:] if part else k_waits[:1]:
            arrive()
        for slot in range(1, NY):
            for pos in blocks:
                qk[place(slot, pos), :] = qy[slot - 1, pos]

    def squares_early():
        gather_q(0)
        wq[...] = dot3((thi[:, :lanes], tlo[:, :lanes]), split(qk[:lanes, :]), 1, 0)
    u_all.wait_recv()
    to_twin.start()
    for half_t in range(2):
        every = tz.at[half_t, pl.ds(0, NZ - 1)]
        t_copy(half_t, 0, every, every).wait_send()

    cut = 512
    parts = (pl.ds(0, cut), pl.ds(cut, width - cut))
    most = NZ // 2
    early = most * rows
    squares_early()
    from_twin.wait_recv()
    known = jnp.concatenate([pp[:most].reshape(early, wide), jnp.zeros((NZ * rows - early, wide), F32)], axis=0)
    hi, lo = split(known.T)
    pthi[...] = hi
    ptlo[...] = lo
    for c in range(2):
        block = dot3((pthi[...], ptlo[...]), (xhi[:, parts[c]], xlo[:, parts[c]]), 1, 0)
        op[:, :, parts[c]] = block.reshape(NY, rows, block.shape[-1])
    from_all[0]()
    from_all[1]()
    late = split(pp[most:].reshape(NZ * rows - early, wide).T)

    def product(c):
        block = dot3(late, (xhi[early:, parts[c]], xlo[early:, parts[c]]), 1, 0)
        op[:, :, parts[c]] = op[:, :, parts[c]] + block.reshape(NY, rows, block.shape[-1])

    def pass_on(way, t, step, h, c):
        w = 0 if way > 0 else 1
        part = op.at[lax.rem(y + way * step + NY, NY), halves(h), parts[c]]
        copy(part, ry.at[w, t, :, parts[c]], ry_s.at[c], ry_r.at[min(t, 1), c], at_y(way)).start()

    def arrived(kind, c):
        here = ry.at[:, 1:3, :, parts[c]] if kind else ry.at[:, 0, :, parts[c]]
        copy(here, here, ry_s.at[c], ry_r.at[kind, c], at_y(1)).wait_recv()

    def begin(c):
        product(c)
        for way in (1, -1):
            pass_on(way, 0, 2, 0 if way > 0 else 1, c)
        for way in (1, -1):
            pass_on(way, 1, 1, 1 if way > 0 else 0, c)

    def finish(c):
        arrived(0, c)
        for way in (1, -1):
            w = h = 0 if way > 0 else 1
            to = lax.rem(y + way + NY, NY)
            op[to, halves(h), parts[c]] = op[to, halves(h), parts[c]] + ry[w, 0, :, parts[c]]
            pass_on(way, 2, 1, h, c)

    def squares_here():
        gather_q(1)
        block = wq[...] + dot3((thi[:, lanes:], tlo[:, lanes:]), split(qk[lanes:, :]), 1, 0)
        block = block * pp[...].reshape(NZ * rows, wide)
        columns = jnp.sum(block.reshape(NZ * rows // 8, 8, wide), axis=0)
        total = columns[:, :128]
        for c in range(1, wide // 128):
            total = total + columns[:, c * 128 : (c + 1) * 128]
        return total

    stages = ((nc, at_col, sqx, qx_s, qx_r), (NZ, at_z, sqz, qz_s, qz_r), (NY, at_y, sqy, qy_s, qy_r))

    def give(stage, total):
        n, device, buf, send_sem, recv_sem = stages[stage]
        sq[stage] = total
        return fan(n, buf, send_sem, recv_sem, lambda s: (sq.at[stage], buf.at[s - 1], device(s)))

    def take(stage, now, total):
        now()
        for one in range(stages[stage][0] - 1):
            total = total + stages[stage][2][one]
        return total

    begin(0)
    total = squares_here()
    now = give(0, total)
    begin(1)
    total = take(0, now, total)
    now = give(1, total)
    finish(0)
    finish(1)
    total = take(1, now, total)
    now = give(2, total)
    for done in closing[:-1]:
        done()
    total = take(2, now, total)
    squares = jnp.sum(jnp.sum(total, axis=1, keepdims=True), axis=0, keepdims=True)
    factor = TARGET_SCALE / jnp.sqrt(squares / (M * N) + EPSILON)

    u_all.wait_send()
    to_twin.wait_send()
    for c in range(2):
        arrived(1, c)
        for h in range(2):
            total = op[y, halves(h), parts[c]] + (ry[0, 2 - h, :, parts[c]] + ry[1, 1 + h, :, parts[c]])
            out_ref[halves(h), parts[c]] = factor * total
    for c in range(2):
        every = ry.at[:, :, :, parts[c]]
        copy(every, every, ry_s.at[c], ry_r.at[0, c], at_y(1)).wait_send()
    closing[-1]()


def body(nc, iterate):
    rows, width = iterate.shape
    sub = rows // nc
    wide = NY * rows
    owned = NY * NZ * sub
    vmem = pltpu.VMEM
    dma = pltpu.SemaphoreType.DMA

    def pair(*shape):
        return [dma(shape), dma(shape)]

    return pl.pallas_call(
        functools.partial(kernel, nc),
        out_shape=vmem((rows, width), F32),
        in_specs=[pl.BlockSpec(memory_space=pl.ANY)],
        out_specs=pl.BlockSpec(memory_space=vmem),
        scratch_shapes=[
            vmem((rows, width), F32),
            vmem((NZ, rows, width), F32),
            vmem((NY, rows, width), F32),
            vmem((NZ * rows, width), BF16),
            vmem((NZ * rows, width), BF16),
            vmem((wide, width), BF16),
            vmem((wide, width), BF16),
            vmem((NZ, rows, wide), F32),
            vmem((nc - 1, NZ, sub, wide), F32),
            vmem((NZ, sub, wide), F32),
            vmem((NY - 1, NZ, sub, wide), F32),
            vmem((owned, wide), F32),
            vmem((2, 2 * rows, owned // 2), F32),
            vmem((2, NZ, rows, owned // 2), F32),
            vmem((NZ * rows, owned), BF16),
            vmem((NZ * rows, owned), BF16),
            vmem((NZ, rows, wide), F32),
            vmem((nc - 1, NZ, sub, wide), F32),
            vmem((NZ, nc // 2, 2, sub, wide), F32),
            vmem((NY - 1, NZ, sub, wide), F32),
            vmem((owned, wide), F32),
            vmem((NZ * rows, wide), F32),
            vmem((wide, NZ * rows), BF16),
            vmem((wide, NZ * rows), BF16),
            vmem((NY, rows, width), F32),
            vmem((2, 3, rows // 2, width), F32),
            vmem((3, 8, 128), F32),
            vmem((nc - 1, 8, 128), F32),
            vmem((NZ - 1, 8, 128), F32),
            vmem((NY - 1, 8, 128), F32),
            dma,
        ]
        + [dma, dma((ring_items(NZ, X_PARTS),))]
        + [dma, dma((ring_items(NY, X_PARTS),))]
        + pair(5)
        + pair(3)
        + [dma((2,)), dma((2, 4))]
        + pair(5)
        + [dma] * 4
        + pair(2)
        + pair(3)
        + [dma((2,)), dma((2, 2))]
        + [dma] * 6,
        compiler_params=pltpu.CompilerParams(
            collective_id=0, has_side_effects=True, vmem_limit_bytes=56 * 1024 * 1024
        ),
    )(iterate)


def solution(mesh):
    return jax.shard_map(
        functools.partial(body, mesh.shape["col"]),
        mesh=mesh,
        in_specs=(P("row", "col"),),
        out_specs=P("row", "col"),
        check_vma=False,
    )
```

```python
import functools
import jax
import jax.numpy as jnp
from jax import lax
from jax.experimental import pallas as pl
from jax.experimental.pallas import tpu as pltpu
from jax.sharding import PartitionSpec as P

M = 2048
N = 7168
NY = 4
NZ = 8
X_PARTS = 4

LINEAR_TERM = 3.4445
CUBIC_TERM = -4.775
QUINTIC_TERM = 2.0315
TARGET_SCALE = 0.2
EPSILON = 1e-07
MESH = pl.DeviceIdType.MESH
F32 = jnp.float32
BF16 = jnp.bfloat16


def split(value):
    high = value.astype(BF16)
    return high, (value - high.astype(F32)).astype(BF16)


def dot3(left, right, left_dim, right_dim):
    return lax.dot_general(
        jnp.concatenate([left[0], left[0], left[1]], axis=left_dim),
        jnp.concatenate([right[0], right[1], right[0]], axis=right_dim),
        (((left_dim,), (right_dim,)), ((), ())),
        preferred_element_type=F32,
    )


class Ring:
    def __init__(self, n, parts, device, src, land, two, every, send_sem, recv_sem):
        self.parts, self.device, self.src, self.land = parts, device, src, land
        self.two, self.every, self.send_sem, self.recv_sem = two, every, send_sem, recv_sem
        self.items = ring_items(n, parts)

    def copy(self, src, dst, t, way):
        return pltpu.make_async_remote_copy(
            src_ref=src,
            dst_ref=dst,
            send_sem=self.send_sem,
            recv_sem=self.recv_sem.at[t],
            device_id=self.device(way),
            device_id_type=MESH,
        )

    def send(self, t):
        for way in (1, -1):
            d, h = t // self.parts, t % self.parts
            h = h if way > 0 else self.parts - 1 - h
            self.copy(self.src(way, d, h), self.land(way, d, h), t, way).start()

    def open(self):
        for t in range(min(self.parts, self.items)):
            self.send(t)

    def take(self, t):
        self.copy(self.two, self.two, t, 1).wait_recv()
        if t + self.parts < self.items:
            self.send(t + self.parts)

    def close(self):
        self.copy(self.every, self.every, 0, 1).wait_send()


def ring_items(n, parts):
    return parts * (n - 1) // 2


def slot_order(n):
    out = [0]
    for s in range(1, n // 2):
        out += [s, n - s]
    return out + [n // 2]


def kernel(
    nc, x_hbm, out_ref,
    xv, xz, xy, xhi, xlo, jhi, jlo, gp, gr, gs, gy, gj, tt, tz, thi, tlo, cp, cr, pp, qy, qk, wq, pthi, ptlo, op, ry,
    sq, sqx, sqz, sqy,
    x_s, xz_s, xz_r, xy_s, xy_r, g_s, g_r, gy_s, gy_r, tz_s, tz_r, c_s, c_r, u_s, u_r, v_s, v_r, p_s, p_r, qk_s, qk_r, ry_s, ry_r,
    qx_s, qx_r, qz_s, qz_r, qy_s, qy_r,
):
    rows, width = xv.shape
    half = rows // 2
    sub = rows // nc
    owned = NZ * sub
    wide = NY * rows
    row, col = lax.axis_index("row"), lax.axis_index("col")
    y, z = lax.div(row, NZ), lax.rem(row, NZ)

    def at_y(step):
        return (lax.rem(y + step + NY, NY) * NZ + z, col)

    def at_z(step):
        return (y * NZ + lax.rem(z + step + NZ, NZ), col)

    nx = nc // 2
    x, core = lax.div(col, 2), lax.rem(col, 2)
    twin = (row, col + 1 - 2 * core)

    def at_x(step):
        return (row, lax.rem(x + step + nx, nx) * 2 + core)

    def at_col(step):
        return (row, lax.rem(col + step, nc))

    def copy(src, dst, send_sem, recv_sem, device):
        return pltpu.make_async_remote_copy(
            src_ref=src, dst_ref=dst, send_sem=send_sem, recv_sem=recv_sem, device_id=device, device_id_type=MESH
        )

    fetch = pltpu.make_async_copy(x_hbm, xv, x_s)
    fetch.start()
    barrier = pltpu.get_barrier_semaphore()
    friends = [at_z(1), at_z(-1), at_y(1), at_y(-1), at_y(2)]
    friends += [at_z(s) for s in range(2, NZ - 1)] + [at_col(s) for s in range(1, nc)]
    for friend in friends:
        pl.semaphore_signal(barrier, inc=1, device_id=friend, device_id_type=MESH)
    pl.semaphore_wait(barrier, len(friends))

    def halves(h):
        return pl.ds(h * half, half)

    def block_ring(n, parts, device, own, buf, send_sem, recv_sem):
        def src(way, d, h):
            return own(h) if d == 0 else buf.at[way * d % n, pl.ds(h * (rows // parts), rows // parts)]

        def land(way, d, h):
            return buf.at[way * (d + 1) % n, pl.ds(h * (rows // parts), rows // parts)]

        two = buf.at[0, pl.ds(0, 2 * (rows // parts))]
        return Ring(n, parts, device, src, land, two, buf.at[pl.ds(0, n - 1)], send_sem, recv_sem)

    def own_x(h):
        return x_hbm.at[pl.ds(h * (rows // X_PARTS), rows // X_PARTS)]

    z_ring = block_ring(NZ, X_PARTS, at_z, own_x, xz, xz_s, xz_r)
    y_ring = block_ring(NY, X_PARTS, at_y, own_x, xy, xy_s, xy_r)
    z_ring.open()
    y_ring.open()
    fetch.wait()
    order = slot_order(NZ)
    closing = []

    def span(first, last):
        return pl.ds(first * rows, (last - first) * rows)

    def keep_j(slot, value):
        where = pl.ds(pl.multiple_of(lax.rem(y - slot + NY, NY) * rows, rows), rows)
        hi, lo = split(value)
        jhi[where, :] = hi
        jlo[where, :] = lo

    def keep_i(pos, value):
        hi, lo = split(value)
        xhi[span(pos, pos + 1), :] = hi
        xlo[span(pos, pos + 1), :] = lo

    def each(n, act):
        for j in sorted(range(1, n), key=lambda j: -min(j, n - j)):
            act(j)

    def fan(n, whole, send_sem, recv_sem, make):
        every = copy(whole, whole, send_sem, recv_sem, twin)
        each(n, lambda j: copy(*make(j)[:2], send_sem, recv_sem, make(j)[2]).start())
        closing.append(every.wait_send)
        return every.wait_recv

    def scatter(part, buf, b, first, last, send_sem, recv_sem):
        def make(j):
            to = at_col(j)
            mine_there = pl.ds(pl.multiple_of(to[1] * sub, sub), sub)
            return part.at[pl.ds(first, last - first), mine_there], buf.at[j - 1, pl.ds(first, last - first)], to

        return fan(nc, buf.at[:, pl.ds(first, last - first)], send_sem.at[b], recv_sem.at[b], make)

    def gathered(part, buf, pos):
        total = part[pos, pl.ds(pl.multiple_of(col * sub, sub), sub), :]
        for j in range(1, nc):
            total = total + buf[j - 1, pos]
        return total

    def spread_y(src, buf, b, first, last, send_sem, recv_sem):
        where = pl.ds(first, last - first)
        return fan(
            NY, buf.at[:, where], send_sem.at[b], recv_sem.at[b], lambda s: (src, buf.at[s - 1, where], at_y(s))
        )

    keep_i(0, xv[...])
    keep_j(0, xv[...])
    y_waits, arrivals = [], []
    spans = ((0, 5), (5, NZ))

    def gram(first, last):
        for pos in range(first, last):
            if pos:
                keep_i(pos, xz[order[pos]])
        where = span(first, last)
        block = dot3((xhi[where, :], xlo[where, :]), (jhi[...], jlo[...]), 1, 1)
        gp[first:last] = block.reshape(last - first, rows, wide)

    y_spans = ((0, 4), (4, 7), (7, NZ))

    def drain_g(b, which):
        first, last = y_spans[b]
        for one in which:
            arrivals[one]()
        for pos in range(first, last):
            gs[pos] = gathered(gp, gr, pos)
        y_waits.append(spread_y(gs.at[pl.ds(first, last - first)], gy, b, first, last, gy_s, gy_r))

    for item in range(z_ring.items):
        z_ring.take(item)
        if item < y_ring.items:
            y_ring.take(item)
        t = (2 * item + 2) / X_PARTS - 1
        if t == 1:
            keep_j(1, xy[1])
            keep_j(NY - 1, xy[NY - 1])
        if t == 2:
            keep_j(2, xy[2])
            gram(0, 3)
            arrivals.append(scatter(gp, gr, 0, 0, 3, g_s, g_r))
        if t == 3:
            gram(3, 4)
            arrivals.append(scatter(gp, gr, 1, 3, 4, g_s, g_r))
        if t == 4:
            gram(4, 5)
            arrivals.append(scatter(gp, gr, 2, 4, 5, g_s, g_r))
            drain_g(0, (0, 1))
        if t == 5:
            gram(5, 7)
            arrivals.append(scatter(gp, gr, 3, 5, 7, g_s, g_r))
        if t == 6:
            gram(7, NZ)
            arrivals.append(scatter(gp, gr, 4, 7, NZ, g_s, g_r))

    group = NY * sub

    def place(slot, pos):
        first = (order[pos] + 1) % NZ * group
        return pl.ds(pl.multiple_of(first + lax.rem(y - slot + NY, NY) * sub, sub), sub)

    def settle(b):
        first, last = y_spans[b]
        for pos in range(first, last):
            gj[place(0, pos), :] = gs[pos]
        y_waits[b]()
        for slot in range(1, NY):
            for pos in range(first, last):
                gj[place(slot, pos), :] = gy[slot - 1, pos]

    pair_of_y, in_pair = lax.div(y, 2), lax.rem(y, 2)
    mine = pl.ds(pl.multiple_of(in_pair * rows, rows), rows)
    lanes = owned * NY // 2
    near = [(0, 1, 1, 0, rows), (0, -1, NZ - 1, 0, rows)]
    last = [(2, 2, 4, 0, half), (NZ - 2, -2, 4, half, half)]
    t_moves = (
        near + [(1, 1, 2, 0, rows), (NZ - 1, -1, NZ - 2, 0, rows), (2, 1, 3, 0, rows), (NZ - 2, -1, NZ - 3, 0, rows)] + last,
        near + [(0, 2, 2, 0, rows), (0, -2, NZ - 2, 0, rows), (2, 1, 3, 0, rows), (NZ - 2, -1, NZ - 3, 0, rows)] + last,
    )

    def t_copy(part, k, src, dst):
        return copy(src, dst, tz_s.at[part], tz_r.at[part, k // 2], at_z(t_moves[part][k][1]))

    def t_start(part, first):
        for k in range(first, first + 2):
            source, _, slot, start, size = t_moves[part][k]
            own = tt.at[part, pl.ds(pl.multiple_of(in_pair * rows + start, half), size)]
            src = tz.at[part, source, pl.ds(start, size)] if source else own
            t_copy(part, k, src, tz.at[part, slot, pl.ds(start, size)]).start()

    def t_wait(part, first):
        two = tz.at[part, pl.ds(0, 2 if first < 6 else 1)]
        t_copy(part, first, two, two).wait_recv()

    def t_open(part):
        columns = pl.ds(pl.multiple_of(pair_of_y * 2 * rows, 2 * rows), 2 * rows)
        tt[part] = gj[pl.ds(part * lanes, lanes), columns].T
        t_start(part, 0)

    settle(0)
    t_open(0)
    drain_g(1, (2, 3))
    drain_g(2, (4,))
    z_ring.close()
    t_wait(0, 0)
    t_start(0, 2)
    settle(1)
    settle(2)
    t_open(1)
    t_start(1, 2)
    t_wait(0, 2)
    t_start(0, 4)
    t_start(0, 6)

    right = split(gj[...])
    k_waits, arrivals = [], []

    def square(first, last):
        for pos in range(first, last):
            slot = order[pos]
            halves_t = [tz[part, slot] if pos else tt[part, mine, :] for part in range(2)]
            whole = jnp.concatenate(halves_t, axis=1)
            hi, lo = split(pltpu.roll(whole, slot * group, 1) if pos else whole)
            thi[span(pos, pos + 1), :] = hi
            tlo[span(pos, pos + 1), :] = lo
        where = span(first, last)
        block = dot3((thi[where, :], tlo[where, :]), right, 1, 0)
        cp[first:last] = block.reshape(last - first, rows, wide)

    def drain_c(first, last, which):
        for one in which:
            arrivals[one]()
        for pos in range(first, last):
            value = CUBIC_TERM * gs[pos] + QUINTIC_TERM * gathered(cp, cr, pos)
            if pos == 0:
                lane = lax.broadcasted_iota(jnp.int32, value.shape, 1)
                diagonal = lax.broadcasted_iota(jnp.int32, value.shape, 0) + (y * rows + col * sub)
                value = value + jnp.where(lane == diagonal, LINEAR_TERM, 0.0)
            pp[pos, x, core] = value

    first_span = pl.ds(0, spans[0][1])
    u_every = pp.at[first_span, pl.ds(0, nx - 1), core]
    u_all = copy(u_every, u_every, u_s, u_r, twin)
    v_mine, v_there = pp.at[first_span, :, core], pp.at[first_span, :, 1 - core]
    to_twin, from_twin = copy(v_mine, v_mine, v_s, v_r, twin), copy(v_there, v_there, v_s, v_r, twin)

    def to_chips():
        part = pp.at[first_span, x, core]
        for j in (2, 1, 3):
            copy(part, part, u_s, u_r, at_x(j)).start()

    def to_all(b, first, last):
        part = pp.at[pl.ds(first, last - first), x, core]
        every = pp.at[pl.ds(0, nc - 1), pl.ds(0, last - first), 0]
        return fan(nc, every, p_s.at[b], p_r.at[b], lambda j: (part, part, at_col(j)))

    old = closing[:]
    closing.clear()
    square(0, 1)
    arrivals.append(scatter(cp, cr, 0, 0, 1, c_s, c_r))
    y_ring.close()
    for done in old:
        done()
    t_wait(1, 0)
    t_wait(1, 2)
    t_start(1, 4)
    t_start(1, 6)
    for b in range(1, 3):
        square(2 * b - 1, 2 * b + 1)
        arrivals.append(scatter(cp, cr, b, 2 * b - 1, 2 * b + 1, c_s, c_r))
    t_wait(0, 4)
    t_wait(1, 4)
    square(5, 7)
    arrivals.append(scatter(cp, cr, 3, 5, 7, c_s, c_r))
    t_wait(0, 6)
    t_wait(1, 6)
    square(7, NZ)
    arrivals.append(scatter(cp, cr, 4, 7, NZ, c_s, c_r))

    def rows_to_y(b, first, last):
        k_waits.append(spread_y(pp.at[pl.ds(first, last - first), x, core], qy, b, first, last, qk_s, qk_r))

    drain_c(0, 5, (0, 1, 2))
    to_chips()
    rows_to_y(0, 0, 5)
    drain_c(5, 7, (3,))
    from_all = [to_all(0, 5, 7)]
    rows_to_y(1, 5, 7)
    drain_c(7, NZ, (4,))
    from_all.append(to_all(1, 7, NZ))
    rows_to_y(2, 7, NZ)

    def gather_q(part):
        blocks = range(4 * part, 4 * part + 4)
        for pos in blocks:
            qk[place(0, pos), :] = pp[pos, x, core]
        for arrive in k_waits[1:] if part else k_waits[:1]:
            arrive()
        for slot in range(1, NY):
            for pos in blocks:
                qk[place(slot, pos), :] = qy[slot - 1, pos]

    def squares_early():
        gather_q(0)
        wq[...] = dot3((thi[:, :lanes], tlo[:, :lanes]), split(qk[:lanes, :]), 1, 0)
    u_all.wait_recv()
    to_twin.start()
    for half_t in range(2):
        every = tz.at[half_t, pl.ds(0, NZ - 1)]
        t_copy(half_t, 0, every, every).wait_send()

    cut = 512
    parts = (pl.ds(0, cut), pl.ds(cut, width - cut))
    most = NZ // 2
    early = most * rows
    squares_early()
    from_twin.wait_recv()
    known = jnp.concatenate([pp[:most].reshape(early, wide), jnp.zeros((NZ * rows - early, wide), F32)], axis=0)
    hi, lo = split(known.T)
    pthi[...] = hi
    ptlo[...] = lo
    for c in range(2):
        block = dot3((pthi[...], ptlo[...]), (xhi[:, parts[c]], xlo[:, parts[c]]), 1, 0)
        op[:, :, parts[c]] = block.reshape(NY, rows, block.shape[-1])
    from_all[0]()
    from_all[1]()
    late = split(pp[most:].reshape(NZ * rows - early, wide).T)

    def product(c):
        block = dot3(late, (xhi[early:, parts[c]], xlo[early:, parts[c]]), 1, 0)
        op[:, :, parts[c]] = op[:, :, parts[c]] + block.reshape(NY, rows, block.shape[-1])

    def pass_on(way, t, step, h, c):
        w = 0 if way > 0 else 1
        part = op.at[lax.rem(y + way * step + NY, NY), halves(h), parts[c]]
        copy(part, ry.at[w, t, :, parts[c]], ry_s.at[c], ry_r.at[min(t, 1), c], at_y(way)).start()

    def arrived(kind, c):
        here = ry.at[:, 1:3, :, parts[c]] if kind else ry.at[:, 0, :, parts[c]]
        copy(here, here, ry_s.at[c], ry_r.at[kind, c], at_y(1)).wait_recv()

    def begin(c):
        product(c)
        for way in (1, -1):
            pass_on(way, 0, 2, 0 if way > 0 else 1, c)
        for way in (1, -1):
            pass_on(way, 1, 1, 1 if way > 0 else 0, c)

    def finish(c):
        arrived(0, c)
        for way in (1, -1):
            w = h = 0 if way > 0 else 1
            to = lax.rem(y + way + NY, NY)
            op[to, halves(h), parts[c]] = op[to, halves(h), parts[c]] + ry[w, 0, :, parts[c]]
            pass_on(way, 2, 1, h, c)

    def squares_here():
        gather_q(1)
        block = wq[...] + dot3((thi[:, lanes:], tlo[:, lanes:]), split(qk[lanes:, :]), 1, 0)
        block = block * pp[...].reshape(NZ * rows, wide)
        columns = jnp.sum(block.reshape(NZ * rows // 8, 8, wide), axis=0)
        total = columns[:, :128]
        for c in range(1, wide // 128):
            total = total + columns[:, c * 128 : (c + 1) * 128]
        return total

    stages = ((nc, at_col, sqx, qx_s, qx_r), (NZ, at_z, sqz, qz_s, qz_r), (NY, at_y, sqy, qy_s, qy_r))

    def give(stage, total):
        n, device, buf, send_sem, recv_sem = stages[stage]
        sq[stage] = total
        return fan(n, buf, send_sem, recv_sem, lambda s: (sq.at[stage], buf.at[s - 1], device(s)))

    def take(stage, now, total):
        now()
        for one in range(stages[stage][0] - 1):
            total = total + stages[stage][2][one]
        return total

    begin(0)
    total = squares_here()
    now = give(0, total)
    begin(1)
    total = take(0, now, total)
    now = give(1, total)
    finish(0)
    total = take(1, now, total)
    now = give(2, total)
    finish(1)
    for done in closing[:-1]:
        done()
    total = take(2, now, total)
    squares = jnp.sum(jnp.sum(total, axis=1, keepdims=True), axis=0, keepdims=True)
    factor = TARGET_SCALE / jnp.sqrt(squares / (M * N) + EPSILON)

    u_all.wait_send()
    to_twin.wait_send()
    for c in range(2):
        arrived(1, c)
        for h in range(2):
            total = op[y, halves(h), parts[c]] + (ry[0, 2 - h, :, parts[c]] + ry[1, 1 + h, :, parts[c]])
            out_ref[halves(h), parts[c]] = factor * total
    for c in range(2):
        every = ry.at[:, :, :, parts[c]]
        copy(every, every, ry_s.at[c], ry_r.at[0, c], at_y(1)).wait_send()
    closing[-1]()


def body(nc, iterate):
    rows, width = iterate.shape
    sub = rows // nc
    wide = NY * rows
    owned = NY * NZ * sub
    vmem = pltpu.VMEM
    dma = pltpu.SemaphoreType.DMA

    def pair(*shape):
        return [dma(shape), dma(shape)]

    return pl.pallas_call(
        functools.partial(kernel, nc),
        out_shape=vmem((rows, width), F32),
        in_specs=[pl.BlockSpec(memory_space=pl.ANY)],
        out_specs=pl.BlockSpec(memory_space=vmem),
        scratch_shapes=[
            vmem((rows, width), F32),
            vmem((NZ, rows, width), F32),
            vmem((NY, rows, width), F32),
            vmem((NZ * rows, width), BF16),
            vmem((NZ * rows, width), BF16),
            vmem((wide, width), BF16),
            vmem((wide, width), BF16),
            vmem((NZ, rows, wide), F32),
            vmem((nc - 1, NZ, sub, wide), F32),
            vmem((NZ, sub, wide), F32),
            vmem((NY - 1, NZ, sub, wide), F32),
            vmem((owned, wide), F32),
            vmem((2, 2 * rows, owned // 2), F32),
            vmem((2, NZ, rows, owned // 2), F32),
            vmem((NZ * rows, owned), BF16),
            vmem((NZ * rows, owned), BF16),
            vmem((NZ, rows, wide), F32),
            vmem((nc - 1, NZ, sub, wide), F32),
            vmem((NZ, nc // 2, 2, sub, wide), F32),
            vmem((NY - 1, NZ, sub, wide), F32),
            vmem((owned, wide), F32),
            vmem((NZ * rows, wide), F32),
            vmem((wide, NZ * rows), BF16),
            vmem((wide, NZ * rows), BF16),
            vmem((NY, rows, width), F32),
            vmem((2, 3, rows // 2, width), F32),
            vmem((3, 8, 128), F32),
            vmem((nc - 1, 8, 128), F32),
            vmem((NZ - 1, 8, 128), F32),
            vmem((NY - 1, 8, 128), F32),
            dma,
        ]
        + [dma, dma((ring_items(NZ, X_PARTS),))]
        + [dma, dma((ring_items(NY, X_PARTS),))]
        + pair(5)
        + pair(3)
        + [dma((2,)), dma((2, 4))]
        + pair(5)
        + [dma] * 4
        + pair(2)
        + pair(3)
        + [dma((2,)), dma((2, 2))]
        + [dma] * 6,
        compiler_params=pltpu.CompilerParams(
            collective_id=0, has_side_effects=True, vmem_limit_bytes=56 * 1024 * 1024
        ),
    )(iterate)


def solution(mesh):
    return jax.shard_map(
        functools.partial(body, mesh.shape["col"]),
        mesh=mesh,
        in_specs=(P("row", "col"),),
        out_specs=P("row", "col"),
        check_vma=False,
    )
```

```python
import functools
import jax
import jax.numpy as jnp
from jax import lax
from jax.experimental import pallas as pl
from jax.experimental.pallas import tpu as pltpu
from jax.sharding import PartitionSpec as P

M = 2048
N = 7168
NY = 4
NZ = 8
X_PARTS = 2

LINEAR_TERM = 3.4445
CUBIC_TERM = -4.775
QUINTIC_TERM = 2.0315
TARGET_SCALE = 0.2
EPSILON = 1e-07
MESH = pl.DeviceIdType.MESH
F32 = jnp.float32
BF16 = jnp.bfloat16


def split(value):
    high = value.astype(BF16)
    return high, (value - high.astype(F32)).astype(BF16)


def dot3(left, right, left_dim, right_dim):
    return lax.dot_general(
        jnp.concatenate([left[0], left[0], left[1]], axis=left_dim),
        jnp.concatenate([right[0], right[1], right[0]], axis=right_dim),
        (((left_dim,), (right_dim,)), ((), ())),
        preferred_element_type=F32,
    )


class Ring:
    def __init__(self, n, parts, device, src, land, two, every, send_sem, recv_sem):
        self.parts, self.device, self.src, self.land = parts, device, src, land
        self.two, self.every, self.send_sem, self.recv_sem = two, every, send_sem, recv_sem
        self.items = ring_items(n, parts)

    def copy(self, src, dst, t, way):
        return pltpu.make_async_remote_copy(
            src_ref=src,
            dst_ref=dst,
            send_sem=self.send_sem,
            recv_sem=self.recv_sem.at[t],
            device_id=self.device(way),
            device_id_type=MESH,
        )

    def send(self, t):
        for way in (1, -1):
            d, h = t // self.parts, t % self.parts
            h = h if way > 0 else self.parts - 1 - h
            self.copy(self.src(way, d, h), self.land(way, d, h), t, way).start()

    def open(self):
        for t in range(min(self.parts, self.items)):
            self.send(t)

    def take(self, t):
        self.copy(self.two, self.two, t, 1).wait_recv()
        if t + self.parts < self.items:
            self.send(t + self.parts)

    def close(self):
        self.copy(self.every, self.every, 0, 1).wait_send()


def ring_items(n, parts):
    return parts * (n - 1) // 2


def slot_order(n):
    out = [0]
    for s in range(1, n // 2):
        out += [s, n - s]
    return out + [n // 2]


def kernel(
    nc, x_hbm, out_ref,
    xv, xz, xy, xhi, xlo, jhi, jlo, gp, gr, gs, gy, gj, tt, tz, thi, tlo, cp, cr, pp, qy, qk, wq, pthi, ptlo, op, ry,
    sq, sqx, sqz, sqy,
    x_s, xz_s, xz_r, xy_s, xy_r, g_s, g_r, gy_s, gy_r, tz_s, tz_r, c_s, c_r, u_s, u_r, v_s, v_r, p_s, p_r, qk_s, qk_r, ry_s, ry_r,
    qx_s, qx_r, qz_s, qz_r, qy_s, qy_r,
):
    rows, width = xv.shape
    half = rows // 2
    sub = rows // nc
    owned = NZ * sub
    wide = NY * rows
    row, col = lax.axis_index("row"), lax.axis_index("col")
    y, z = lax.div(row, NZ), lax.rem(row, NZ)

    def at_y(step):
        return (lax.rem(y + step + NY, NY) * NZ + z, col)

    def at_z(step):
        return (y * NZ + lax.rem(z + step + NZ, NZ), col)

    nx = nc // 2
    x, core = lax.div(col, 2), lax.rem(col, 2)
    twin = (row, col + 1 - 2 * core)

    def at_x(step):
        return (row, lax.rem(x + step + nx, nx) * 2 + core)

    def at_col(step):
        return (row, lax.rem(col + step, nc))

    def copy(src, dst, send_sem, recv_sem, device):
        return pltpu.make_async_remote_copy(
            src_ref=src, dst_ref=dst, send_sem=send_sem, recv_sem=recv_sem, device_id=device, device_id_type=MESH
        )

    fetch = pltpu.make_async_copy(x_hbm, xv, x_s)
    fetch.start()
    barrier = pltpu.get_barrier_semaphore()
    friends = [at_z(1), at_z(-1), at_y(1), at_y(-1), at_y(2)]
    friends += [at_z(s) for s in range(2, NZ - 1)] + [at_col(s) for s in range(1, nc)]
    for friend in friends:
        pl.semaphore_signal(barrier, inc=1, device_id=friend, device_id_type=MESH)
    pl.semaphore_wait(barrier, len(friends))

    def halves(h):
        return pl.ds(h * half, half)

    def block_ring(n, parts, device, own, buf, send_sem, recv_sem):
        def src(way, d, h):
            return own(h) if d == 0 else buf.at[way * d % n, pl.ds(h * (rows // parts), rows // parts)]

        def land(way, d, h):
            return buf.at[way * (d + 1) % n, pl.ds(h * (rows // parts), rows // parts)]

        two = buf.at[0, pl.ds(0, 2 * (rows // parts))]
        return Ring(n, parts, device, src, land, two, buf.at[pl.ds(0, n - 1)], send_sem, recv_sem)

    def own_x(h):
        return x_hbm.at[pl.ds(h * (rows // X_PARTS), rows // X_PARTS)]

    z_ring = block_ring(NZ, X_PARTS, at_z, own_x, xz, xz_s, xz_r)
    y_ring = block_ring(NY, X_PARTS, at_y, own_x, xy, xy_s, xy_r)
    z_ring.open()
    y_ring.open()
    fetch.wait()
    order = slot_order(NZ)
    closing = []

    def span(first, last):
        return pl.ds(first * rows, (last - first) * rows)

    def keep_j(slot, value):
        where = pl.ds(pl.multiple_of(lax.rem(y - slot + NY, NY) * rows, rows), rows)
        hi, lo = split(value)
        jhi[where, :] = hi
        jlo[where, :] = lo

    def keep_i(pos, value):
        hi, lo = split(value)
        xhi[span(pos, pos + 1), :] = hi
        xlo[span(pos, pos + 1), :] = lo

    def each(n, act):
        for j in sorted(range(1, n), key=lambda j: -min(j, n - j)):
            act(j)

    def fan(n, whole, send_sem, recv_sem, make):
        every = copy(whole, whole, send_sem, recv_sem, twin)
        each(n, lambda j: copy(*make(j)[:2], send_sem, recv_sem, make(j)[2]).start())
        closing.append(every.wait_send)
        return every.wait_recv

    def scatter(part, buf, b, first, last, send_sem, recv_sem):
        def make(j):
            to = at_col(j)
            mine_there = pl.ds(pl.multiple_of(to[1] * sub, sub), sub)
            return part.at[pl.ds(first, last - first), mine_there], buf.at[j - 1, pl.ds(first, last - first)], to

        return fan(nc, buf.at[:, pl.ds(first, last - first)], send_sem.at[b], recv_sem.at[b], make)

    def gathered(part, buf, pos):
        total = part[pos, pl.ds(pl.multiple_of(col * sub, sub), sub), :]
        for j in range(1, nc):
            total = total + buf[j - 1, pos]
        return total

    def spread_y(src, buf, b, first, last, send_sem, recv_sem):
        where = pl.ds(first, last - first)
        return fan(
            NY, buf.at[:, where], send_sem.at[b], recv_sem.at[b], lambda s: (src, buf.at[s - 1, where], at_y(s))
        )

    keep_i(0, xv[...])
    keep_j(0, xv[...])
    y_waits, arrivals = [], []
    spans = ((0, 5), (5, NZ))

    def gram(first, last):
        for pos in range(first, last):
            if pos:
                keep_i(pos, xz[order[pos]])
        where = span(first, last)
        block = dot3((xhi[where, :], xlo[where, :]), (jhi[...], jlo[...]), 1, 1)
        gp[first:last] = block.reshape(last - first, rows, wide)

    y_spans = ((0, 4), (4, 7), (7, NZ))

    def drain_g(b, which):
        first, last = y_spans[b]
        for one in which:
            arrivals[one]()
        for pos in range(first, last):
            gs[pos] = gathered(gp, gr, pos)
        y_waits.append(spread_y(gs.at[pl.ds(first, last - first)], gy, b, first, last, gy_s, gy_r))

    for item in range(z_ring.items):
        z_ring.take(item)
        if item < y_ring.items:
            y_ring.take(item)
        t = (2 * item + 2) / X_PARTS - 1
        if t == 1:
            keep_j(1, xy[1])
            keep_j(NY - 1, xy[NY - 1])
        if t == 2:
            keep_j(2, xy[2])
            gram(0, 3)
            arrivals.append(scatter(gp, gr, 0, 0, 3, g_s, g_r))
        if t == 3:
            gram(3, 4)
            arrivals.append(scatter(gp, gr, 1, 3, 4, g_s, g_r))
        if t == 4:
            gram(4, 5)
            arrivals.append(scatter(gp, gr, 2, 4, 5, g_s, g_r))
            drain_g(0, (0, 1))
        if t == 5:
            gram(5, 7)
            arrivals.append(scatter(gp, gr, 3, 5, 7, g_s, g_r))
        if t == 6:
            gram(7, NZ)
            arrivals.append(scatter(gp, gr, 4, 7, NZ, g_s, g_r))

    group = NY * sub

    def place(slot, pos):
        first = (order[pos] + 1) % NZ * group
        return pl.ds(pl.multiple_of(first + lax.rem(y - slot + NY, NY) * sub, sub), sub)

    def settle(b):
        first, last = y_spans[b]
        for pos in range(first, last):
            gj[place(0, pos), :] = gs[pos]
        y_waits[b]()
        for slot in range(1, NY):
            for pos in range(first, last):
                gj[place(slot, pos), :] = gy[slot - 1, pos]

    pair_of_y, in_pair = lax.div(y, 2), lax.rem(y, 2)
    mine = pl.ds(pl.multiple_of(in_pair * rows, rows), rows)
    lanes = owned * NY // 2
    near = [(0, 1, 1, 0, rows), (0, -1, NZ - 1, 0, rows)]
    last = [(2, 2, 4, 0, half), (NZ - 2, -2, 4, half, half)]
    t_moves = (
        near + [(1, 1, 2, 0, rows), (NZ - 1, -1, NZ - 2, 0, rows), (2, 1, 3, 0, rows), (NZ - 2, -1, NZ - 3, 0, rows)] + last,
        near + [(0, 2, 2, 0, rows), (0, -2, NZ - 2, 0, rows), (2, 1, 3, 0, rows), (NZ - 2, -1, NZ - 3, 0, rows)] + last,
    )

    def t_copy(part, k, src, dst):
        return copy(src, dst, tz_s.at[part], tz_r.at[part, k // 2], at_z(t_moves[part][k][1]))

    def t_start(part, first):
        for k in range(first, first + 2):
            source, _, slot, start, size = t_moves[part][k]
            own = tt.at[part, pl.ds(pl.multiple_of(in_pair * rows + start, half), size)]
            src = tz.at[part, source, pl.ds(start, size)] if source else own
            t_copy(part, k, src, tz.at[part, slot, pl.ds(start, size)]).start()

    def t_wait(part, first):
        two = tz.at[part, pl.ds(0, 2 if first < 6 else 1)]
        t_copy(part, first, two, two).wait_recv()

    def t_open(part):
        columns = pl.ds(pl.multiple_of(pair_of_y * 2 * rows, 2 * rows), 2 * rows)
        tt[part] = gj[pl.ds(part * lanes, lanes), columns].T
        t_start(part, 0)

    settle(0)
    t_open(0)
    drain_g(1, (2, 3))
    drain_g(2, (4,))
    z_ring.close()
    t_wait(0, 0)
    t_start(0, 2)
    settle(1)
    settle(2)
    t_open(1)
    t_start(1, 2)
    t_wait(0, 2)
    t_start(0, 4)
    t_start(0, 6)

    right = split(gj[...])
    k_waits, arrivals = [], []

    def square(first, last):
        for pos in range(first, last):
            slot = order[pos]
            halves_t = [tz[part, slot] if pos else tt[part, mine, :] for part in range(2)]
            whole = jnp.concatenate(halves_t, axis=1)
            hi, lo = split(pltpu.roll(whole, slot * group, 1) if pos else whole)
            thi[span(pos, pos + 1), :] = hi
            tlo[span(pos, pos + 1), :] = lo
        where = span(first, last)
        block = dot3((thi[where, :], tlo[where, :]), right, 1, 0)
        cp[first:last] = block.reshape(last - first, rows, wide)

    def drain_c(first, last, which):
        for one in which:
            arrivals[one]()
        for pos in range(first, last):
            value = CUBIC_TERM * gs[pos] + QUINTIC_TERM * gathered(cp, cr, pos)
            if pos == 0:
                lane = lax.broadcasted_iota(jnp.int32, value.shape, 1)
                diagonal = lax.broadcasted_iota(jnp.int32, value.shape, 0) + (y * rows + col * sub)
                value = value + jnp.where(lane == diagonal, LINEAR_TERM, 0.0)
            pp[pos, x, core] = value

    first_span = pl.ds(0, spans[0][1])
    u_every = pp.at[first_span, pl.ds(0, nx - 1), core]
    u_all = copy(u_every, u_every, u_s, u_r, twin)
    v_mine, v_there = pp.at[first_span, :, core], pp.at[first_span, :, 1 - core]
    to_twin, from_twin = copy(v_mine, v_mine, v_s, v_r, twin), copy(v_there, v_there, v_s, v_r, twin)

    def to_chips():
        part = pp.at[first_span, x, core]
        for j in (2, 1, 3):
            copy(part, part, u_s, u_r, at_x(j)).start()

    def to_all(b, first, last):
        part = pp.at[pl.ds(first, last - first), x, core]
        every = pp.at[pl.ds(0, nc - 1), pl.ds(0, last - first), 0]
        return fan(nc, every, p_s.at[b], p_r.at[b], lambda j: (part, part, at_col(j)))

    old = closing[:]
    closing.clear()
    square(0, 1)
    arrivals.append(scatter(cp, cr, 0, 0, 1, c_s, c_r))
    y_ring.close()
    for done in old:
        done()
    t_wait(1, 0)
    t_wait(1, 2)
    t_start(1, 4)
    t_start(1, 6)
    for b in range(1, 3):
        square(2 * b - 1, 2 * b + 1)
        arrivals.append(scatter(cp, cr, b, 2 * b - 1, 2 * b + 1, c_s, c_r))
    t_wait(0, 4)
    t_wait(1, 4)
    square(5, 7)
    arrivals.append(scatter(cp, cr, 3, 5, 7, c_s, c_r))
    t_wait(0, 6)
    t_wait(1, 6)
    square(7, NZ)
    arrivals.append(scatter(cp, cr, 4, 7, NZ, c_s, c_r))

    def rows_to_y(b, first, last):
        k_waits.append(spread_y(pp.at[pl.ds(first, last - first), x, core], qy, b, first, last, qk_s, qk_r))

    drain_c(0, 5, (0, 1, 2))
    to_chips()
    rows_to_y(0, 0, 5)
    drain_c(5, 7, (3,))
    from_all = [to_all(0, 5, 7)]
    rows_to_y(1, 5, 7)
    drain_c(7, NZ, (4,))
    from_all.append(to_all(1, 7, NZ))
    rows_to_y(2, 7, NZ)

    def gather_q(part):
        blocks = range(4 * part, 4 * part + 4)
        for pos in blocks:
            qk[place(0, pos), :] = pp[pos, x, core]
        for arrive in k_waits[1:] if part else k_waits[:1]:
            arrive()
        for slot in range(1, NY):
            for pos in blocks:
                qk[place(slot, pos), :] = qy[slot - 1, pos]

    def squares_early():
        gather_q(0)
        wq[...] = dot3((thi[:, :lanes], tlo[:, :lanes]), split(qk[:lanes, :]), 1, 0)
    u_all.wait_recv()
    to_twin.start()
    for half_t in range(2):
        every = tz.at[half_t, pl.ds(0, NZ - 1)]
        t_copy(half_t, 0, every, every).wait_send()

    cut = 512
    parts = (pl.ds(0, cut), pl.ds(cut, width - cut))
    most = NZ // 2
    early = most * rows
    squares_early()
    from_twin.wait_recv()
    known = jnp.concatenate([pp[:most].reshape(early, wide), jnp.zeros((NZ * rows - early, wide), F32)], axis=0)
    hi, lo = split(known.T)
    pthi[...] = hi
    ptlo[...] = lo
    for c in range(2):
        block = dot3((pthi[...], ptlo[...]), (xhi[:, parts[c]], xlo[:, parts[c]]), 1, 0)
        op[:, :, parts[c]] = block.reshape(NY, rows, block.shape[-1])
    from_all[0]()
    from_all[1]()
    late = split(pp[most:].reshape(NZ * rows - early, wide).T)

    def product(c):
        block = dot3(late, (xhi[early:, parts[c]], xlo[early:, parts[c]]), 1, 0)
        op[:, :, parts[c]] = op[:, :, parts[c]] + block.reshape(NY, rows, block.shape[-1])

    def pass_on(way, t, step, h, c):
        w = 0 if way > 0 else 1
        part = op.at[lax.rem(y + way * step + NY, NY), halves(h), parts[c]]
        copy(part, ry.at[w, t, :, parts[c]], ry_s.at[c], ry_r.at[min(t, 1), c], at_y(way)).start()

    def arrived(kind, c):
        here = ry.at[:, 1:3, :, parts[c]] if kind else ry.at[:, 0, :, parts[c]]
        copy(here, here, ry_s.at[c], ry_r.at[kind, c], at_y(1)).wait_recv()

    def begin(c):
        product(c)
        for way in (1, -1):
            pass_on(way, 0, 2, 0 if way > 0 else 1, c)
        for way in (1, -1):
            pass_on(way, 1, 1, 1 if way > 0 else 0, c)

    def finish(c):
        arrived(0, c)
        for way in (1, -1):
            w = h = 0 if way > 0 else 1
            to = lax.rem(y + way + NY, NY)
            op[to, halves(h), parts[c]] = op[to, halves(h), parts[c]] + ry[w, 0, :, parts[c]]
            pass_on(way, 2, 1, h, c)

    def squares_here():
        gather_q(1)
        block = wq[...] + dot3((thi[:, lanes:], tlo[:, lanes:]), split(qk[lanes:, :]), 1, 0)
        block = block * pp[...].reshape(NZ * rows, wide)
        columns = jnp.sum(block.reshape(NZ * rows // 8, 8, wide), axis=0)
        total = columns[:, :128]
        for c in range(1, wide // 128):
            total = total + columns[:, c * 128 : (c + 1) * 128]
        return total

    stages = ((nc, at_col, sqx, qx_s, qx_r), (NZ, at_z, sqz, qz_s, qz_r), (NY, at_y, sqy, qy_s, qy_r))

    def give(stage, total):
        n, device, buf, send_sem, recv_sem = stages[stage]
        sq[stage] = total
        return fan(n, buf, send_sem, recv_sem, lambda s: (sq.at[stage], buf.at[s - 1], device(s)))

    def take(stage, now, total):
        now()
        for one in range(stages[stage][0] - 1):
            total = total + stages[stage][2][one]
        return total

    begin(0)
    total = squares_here()
    now = give(0, total)
    begin(1)
    total = take(0, now, total)
    now = give(1, total)
    finish(0)
    finish(1)
    total = take(1, now, total)
    now = give(2, total)
    for done in closing[:-1]:
        done()
    total = take(2, now, total)
    squares = jnp.sum(jnp.sum(total, axis=1, keepdims=True), axis=0, keepdims=True)
    factor = TARGET_SCALE / jnp.sqrt(squares / (M * N) + EPSILON)

    u_all.wait_send()
    to_twin.wait_send()
    for c in range(2):
        arrived(1, c)
        for h in range(2):
            total = op[y, halves(h), parts[c]] + (ry[0, 2 - h, :, parts[c]] + ry[1, 1 + h, :, parts[c]])
            out_ref[halves(h), parts[c]] = factor * total
    for c in range(2):
        every = ry.at[:, :, :, parts[c]]
        copy(every, every, ry_s.at[c], ry_r.at[0, c], at_y(1)).wait_send()
    closing[-1]()


def body(nc, iterate):
    rows, width = iterate.shape
    sub = rows // nc
    wide = NY * rows
    owned = NY * NZ * sub
    vmem = pltpu.VMEM
    dma = pltpu.SemaphoreType.DMA

    def pair(*shape):
        return [dma(shape), dma(shape)]

    return pl.pallas_call(
        functools.partial(kernel, nc),
        out_shape=vmem((rows, width), F32),
        in_specs=[pl.BlockSpec(memory_space=pl.ANY)],
        out_specs=pl.BlockSpec(memory_space=vmem),
        scratch_shapes=[
            vmem((rows, width), F32),
            vmem((NZ, rows, width), F32),
            vmem((NY, rows, width), F32),
            vmem((NZ * rows, width), BF16),
            vmem((NZ * rows, width), BF16),
            vmem((wide, width), BF16),
            vmem((wide, width), BF16),
            vmem((NZ, rows, wide), F32),
            vmem((nc - 1, NZ, sub, wide), F32),
            vmem((NZ, sub, wide), F32),
            vmem((NY - 1, NZ, sub, wide), F32),
            vmem((owned, wide), F32),
            vmem((2, 2 * rows, owned // 2), F32),
            vmem((2, NZ, rows, owned // 2), F32),
            vmem((NZ * rows, owned), BF16),
            vmem((NZ * rows, owned), BF16),
            vmem((NZ, rows, wide), F32),
            vmem((nc - 1, NZ, sub, wide), F32),
            vmem((NZ, nc // 2, 2, sub, wide), F32),
            vmem((NY - 1, NZ, sub, wide), F32),
            vmem((owned, wide), F32),
            vmem((NZ * rows, wide), F32),
            vmem((wide, NZ * rows), BF16),
            vmem((wide, NZ * rows), BF16),
            vmem((NY, rows, width), F32),
            vmem((2, 3, rows // 2, width), F32),
            vmem((3, 8, 128), F32),
            vmem((nc - 1, 8, 128), F32),
            vmem((NZ - 1, 8, 128), F32),
            vmem((NY - 1, 8, 128), F32),
            dma,
        ]
        + [dma, dma((ring_items(NZ, X_PARTS),))]
        + [dma, dma((ring_items(NY, X_PARTS),))]
        + pair(5)
        + pair(3)
        + [dma((2,)), dma((2, 4))]
        + pair(5)
        + [dma] * 4
        + pair(2)
        + pair(3)
        + [dma((2,)), dma((2, 2))]
        + [dma] * 6,
        compiler_params=pltpu.CompilerParams(
            collective_id=0, has_side_effects=True, vmem_limit_bytes=56 * 1024 * 1024
        ),
    )(iterate)


def solution(mesh):
    return jax.shard_map(
        functools.partial(body, mesh.shape["col"]),
        mesh=mesh,
        in_specs=(P("row", "col"),),
        out_specs=P("row", "col"),
        check_vma=False,
    )
```
